512 devices in a mesh: seq: 64 (over y, z), head: 8 (over x, core).
Axes of the slice: x: 4, y: 8, z: 8, core: 2. Of those that a mesh axis runs over, the one named last changes fastest.
Arguments:
- enc_rows: bfloat16 [36864, 1024], P('seq', 'head'), may hold values from -1.5 to 1.5
- boundary_flags: int32 [36864], P('seq'), may hold values from 0 to 1, as said below
- boundary_prob: bfloat16 [36864], P('seq'), may hold values from 0.0001 to 0.99
- pad_vector: float32 [1024], replicated, may hold values from -6 to 6
- norm_gain: float32 [1024], replicated, may hold values from 0.25 to 1.75
- w_in: bfloat16 [1024, 10240], P(None, 'head'), may hold values from -0.125 to 0.125
- w_dt: bfloat16 [1024, 64], P(None, 'head'), may hold values from -0.125 to 0.125
- pad_proj: float32 [10240], P('head'), may hold values from -4 to 4
- pad_dt: float32 [64], P('head'), may hold values from -4 to 4
- dt_bias: float32 [64], P('head'), may hold values from -4 to -1
- a_log: float32 [64], P('head'), may hold values from -8.1 to -0.7
- d_skip: float32 [64], P('head'), may hold values from 0.5 to 1.5
- gate_gain: float32 [4096], P('head'), may hold values from 0.25 to 1.75
- w_out: bfloat16 [4096, 1024], P('head'), may hold values from -0.125 to 0.125
Outputs:
- decoded: bfloat16 [36864, 1024], P('seq', 'head')
The draws below stay inside these ranges and needn't reach their ends.
Inputs may be any that keep to these rules, and one draw needn't show every extreme that they name: `boundary_flags`: exactly 9216 flags are 1; the 576 bytes of one index of seq hold at most 432 ones, and those of some index hold exactly 432. The first 18432 bytes hold no ones.
All inputs are finite; a program needn't handle non-finite values.
Results may differ from the reference program's by a relative error of at most 0.0096.
The reference program's roundings to bfloat16 on the way (of `stretch_rows`, `stretch_prob`, `normed`, `mixed` and `main_out`) count: a program that leaves them out, or rounds other values in their place, can miss the bound.
Values may be sent and summed in bfloat16 or wider, within the bound.
No kernel may reach another device: no remote copies, remote signals or barrier semaphores. Data moves between devices by JAX's collectives and lax.ppermute only.
A program may use at most 64 MiB of HBM per device.

```python
import jax
import jax.numpy as jnp
from jax import lax

D = 1024
E = 2048
HEADS = 64
P_SIZE = 64
N = 128
GROUPS = 8
GROUP_COLS = 1280
COLS = 10240
CH_DEV = 144
BYTES_DEV = 576
TOTAL_BYTE_COUNT = 36864
STRETCHES = 9216


def draw_boundary_flags(key, part):
    key = jax.random.fold_in(key, 7)
    shard_total = TOTAL_BYTE_COUNT // BYTES_DEV
    half_total = shard_total // 2
    mean_count = CH_DEV
    key_delta, key_order, key_place = jax.random.split(key, 3)
    pair_count = (half_total - 2) // 2
    shifts = jax.random.randint(key_delta, (pair_count,), -(mean_count - 1), mean_count)
    paired = jnp.stack([2 * mean_count + shifts, 2 * mean_count - shifts], axis=1).reshape(-1)
    leading = jnp.array([3 * mean_count, mean_count], jnp.int32)
    listed = jnp.concatenate([leading, paired.astype(jnp.int32)])
    shard_order = jax.random.permutation(key_order, half_total)
    later_counts = jnp.zeros((half_total,), jnp.int32).at[shard_order].set(listed)
    shard_counts = jnp.concatenate([jnp.zeros((half_total,), jnp.int32), later_counts])
    place_keys = jax.random.split(key_place, shard_total)
    byte_ranks = jax.vmap(lambda single_key: jax.random.permutation(single_key, BYTES_DEV))(place_keys)
    return (byte_ranks < shard_counts[:, None]).astype(jnp.int32).reshape(-1)


def draw_a_log(key, part):
    key = jax.random.fold_in(key, 13)
    return jax.random.uniform(key, (HEADS,), jnp.float32, -8.1, -0.7)


def draw_pad_vector(key, part):
    key = jax.random.fold_in(key, 19)
    key_scale, key_value = jax.random.split(key)
    level = jax.random.uniform(key_scale, (), jnp.float32, 0.5, 1.5)
    return level * jnp.clip(jax.random.normal(key_value, (E - D,), jnp.float32), -4.0, 4.0)


def draw_boundary_prob(key, part):
    key = jax.random.fold_in(key, 23)
    return jax.random.uniform(key, (TOTAL_BYTE_COUNT,), jnp.float32, 0.5, 0.99).astype(jnp.bfloat16)


def draw_enc_rows(key, part):
    key = jax.random.fold_in(key, 29)
    key_rough = jax.random.fold_in(key, 0)
    return jnp.clip(0.25 * jax.random.normal(key_rough, (TOTAL_BYTE_COUNT, D), jnp.float32), -1.5, 1.5).astype(jnp.bfloat16)


def spiked(result, rng, source, target, blocks, factor):
    owner, partner = [(jnp.arange(result.shape[dim]) // (result.shape[dim] // blocks)).reshape([-1 if axis == dim else 1 for axis in range(result.ndim)]) for dim in (source, target)]
    chosen = jax.random.permutation(rng, blocks)[partner]
    strong = (owner == chosen) | (owner == (partner + blocks // 2) % blocks)
    return jnp.where(strong, factor * result, result)


def levels(key, shape, cuts, smallest, top_value):
    def one(axis_at, parts):
        heights = jax.random.uniform(jax.random.fold_in(jax.random.fold_in(key, 6), axis_at), (parts,), jnp.float32, smallest / len(cuts), top_value / len(cuts))
        return jnp.repeat(jnp.exp(heights), shape[axis_at] // parts).reshape((-1,) + (1,) * (len(shape) - axis_at - 1))

    factor_of = one(*cuts[0])
    for cut in cuts[1:]:
        factor_of = factor_of * one(*cut)
    return factor_of


def gaussian(rng, extent, scale, most, cuts=(), kind=jnp.bfloat16):
    values = scale * jax.random.normal(rng, extent, jnp.float32)
    if cuts:
        values = values * levels(rng, extent, cuts, -0.22, 0.18)
    return jnp.clip(values, -most, most).astype(kind)


def heavy_noise(own_key, dims, scale, bound, cuts, heavy, dtype=jnp.bfloat16):
    entries = scale * jax.random.normal(own_key, dims, jnp.float32)
    if cuts:
        entries = entries * levels(own_key, dims, cuts, -0.22, 0.18)
    return jnp.clip(spiked(entries, jax.random.fold_in(own_key, 3), *heavy), -bound, bound).astype(dtype)


def setup_inputs(seed: int = 0) -> dict:
    keys = jax.random.split(jax.random.key(seed), 15)
    enc_rows = draw_enc_rows(jax.random.fold_in(keys[14], 71), 0)
    boundary_flags = draw_boundary_flags(jax.random.fold_in(keys[14], 71), 0)
    boundary_prob = draw_boundary_prob(jax.random.fold_in(keys[14], 71), 0)
    pad_vector = draw_pad_vector(jax.random.fold_in(keys[14], 71), 0)
    norm_gain = jnp.clip(1.0 + 0.15 * jax.random.normal(keys[4], (D,), jnp.float32), 0.25, 1.75)
    w_in = gaussian(keys[5], (D, COLS), E ** -0.5, 0.125, ((1, 8),))
    w_dt = gaussian(keys[6], (D, HEADS), E ** -0.5, 0.125, ((1, 8),))
    pad_proj = gaussian(keys[7], (COLS,), 0.7, 4.0, ((0, 8),), jnp.float32)
    pad_dt = gaussian(keys[8], (HEADS,), 0.7, 4.0, ((0, 8),), jnp.float32)
    dt_bias = jnp.clip(-4.0 + 3.0 * jax.random.uniform(keys[9], (HEADS,), jnp.float32) ** levels(keys[9], (HEADS,), ((0, 8),), -0.2, 0.2), -4.0, -1.0)
    a_log = draw_a_log(jax.random.fold_in(keys[14], 71), 0)
    d_skip = jnp.clip(0.5 + 1.0 * jax.random.uniform(keys[11], (HEADS,), jnp.float32) ** levels(keys[11], (HEADS,), ((0, 8),), -0.2, 0.2), 0.5, 1.5)
    gate_gain = jnp.clip(1.0 + 0.15 * jax.random.normal(keys[12], (HEADS * P_SIZE,), jnp.float32), 0.25, 1.75)
    w_out = heavy_noise(keys[13], (HEADS * P_SIZE, D), (HEADS * P_SIZE) ** -0.5, 0.125, ((0, 8),), (0, 1, 8, 2.0))
    return dict(enc_rows=enc_rows, boundary_flags=boundary_flags, boundary_prob=boundary_prob, pad_vector=pad_vector, norm_gain=norm_gain, w_in=w_in, w_dt=w_dt, pad_proj=pad_proj, pad_dt=pad_dt, dt_bias=dt_bias, a_log=a_log, d_skip=d_skip, gate_gain=gate_gain, w_out=w_out)


eps = 1e-05
highest = lax.Precision.HIGHEST

def state_block(inputs, step_sizes, b_proj, c_proj, decay_rates):
    log_decay = -decay_rates[None] * step_sizes
    running = jnp.cumsum(log_decay, axis=0)
    length = inputs.shape[0]
    lower_mask = jnp.arange(length)[:, None] >= jnp.arange(length)[None, :]
    by_head = jnp.transpose(running, (1, 2, 0))
    spread = by_head[:, :, :, None] - by_head[:, :, None, :]
    decay_mask = jnp.exp(jnp.where(lower_mask, spread, -jnp.inf))
    intersection = jnp.einsum('ign,jgn->gij', c_proj, b_proj, precision=highest)
    weights = intersection[:, None] * decay_mask * jnp.transpose(step_sizes, (1, 2, 0))[:, :, None, :]
    local_out = jnp.einsum('gkij,jgkp->igkp', weights, inputs, precision=highest)
    tail_weight = jnp.exp(running[-1][None] - running) * step_sizes
    local_state = jnp.einsum('jgk,jgkp,jgn->gkpn', tail_weight, inputs, b_proj, precision=highest)
    return (local_out, running, local_state, jnp.exp(running[-1]))

def carried_out(c_proj, running, state_in):
    return jnp.exp(running)[..., None] * jnp.einsum('ign,gkpn->igkp', c_proj, state_in, precision=highest)

def normalize(rows_half, pad_vector, norm_gain):
    rows_wide = rows_half.astype(jnp.float32)
    energy = lax.optimization_barrier(jnp.sum(rows_wide * rows_wide, axis=1)) + jnp.sum(pad_vector * pad_vector)
    inverse = lax.rsqrt(energy / E + eps)
    normed = (rows_wide * inverse[:, None] * norm_gain[None, :]).astype(jnp.bfloat16)
    return (normed, inverse)

def project(normed, inverse, w_in, w_dt, pad_proj, pad_dt, dt_bias):
    projected = jnp.dot(normed, w_in, preferred_element_type=jnp.float32) + inverse[:, None] * pad_proj[None, :]
    step_raw = jnp.dot(normed, w_dt, preferred_element_type=jnp.float32) + inverse[:, None] * pad_dt[None, :] + dt_bias[None, :]
    return (projected, jax.nn.softplus(step_raw))

def split_columns(projected, group_count):
    rows_here = projected.shape[0]
    group_heads = HEADS // GROUPS
    inner_width = group_heads * P_SIZE
    shaped = projected.reshape(rows_here, group_count, 2 * inner_width + 2 * N)
    gate_part = shaped[:, :, :inner_width].reshape(rows_here, group_count, group_heads, P_SIZE)
    inner_part = shaped[:, :, inner_width:2 * inner_width].reshape(rows_here, group_count, group_heads, P_SIZE)
    b_proj = shaped[:, :, 2 * inner_width:2 * inner_width + N]
    c_proj = shaped[:, :, 2 * inner_width + N:]
    return (gate_part, inner_part, b_proj, c_proj)

def gated_norm(gate_part, ssm_out, gate_gain):
    gated = ssm_out * jax.nn.silu(gate_part)
    power = lax.optimization_barrier(jnp.mean(gated * gated, axis=(2, 3)))
    shaped_gain = gate_gain.reshape(1, gated.shape[1], gated.shape[2], gated.shape[3])
    scaled = gated * lax.rsqrt(power + eps)[:, :, None, None] * shaped_gain
    return scaled.astype(jnp.bfloat16).reshape(gated.shape[0], -1)

def reference(enc_rows, boundary_flags, boundary_prob, pad_vector, norm_gain, w_in, w_dt, pad_proj, pad_dt, dt_bias, a_log, d_skip, gate_gain, w_out):
    stretch_id = (jnp.cumsum(boundary_flags) - 1).astype(jnp.int32)
    target = jnp.where(boundary_flags > 0, stretch_id, STRETCHES).astype(jnp.int32)
    stretch_rows = jnp.zeros((STRETCHES + 1, D), jnp.bfloat16).at[target].set(enc_rows)[:STRETCHES]
    stretch_prob = jnp.zeros((STRETCHES + 1,), jnp.bfloat16).at[target].set(boundary_prob)[:STRETCHES]
    normed, inverse = normalize(stretch_rows, pad_vector, norm_gain)
    group_heads = HEADS // GROUPS
    blocks = STRETCHES // CH_DEV

    def one_group(summed, group_params):
        w_in_g, w_dt_g, pad_proj_g, pad_dt_g, bias_g, log_rate_g, skip_g, gain_g, w_out_g = group_params
        projected, step_sizes = project(normed, inverse, w_in_g, w_dt_g, pad_proj_g, pad_dt_g, bias_g)
        gate_part, inner_part, b_proj, c_proj = split_columns(projected, 1)
        decay_rates = jnp.exp(log_rate_g).reshape(1, group_heads)

        def one_block(state_now, pieces):
            inner_b, steps_b, b_block, c_block = pieces
            local_out, running, local_state, total_decay = state_block(inner_b, steps_b, b_block, c_block, decay_rates)
            block_out = local_out + carried_out(c_block, running, state_now)
            state_next = total_decay[..., None, None] * state_now + local_state
            return (state_next, block_out)
        start_state = jnp.zeros((1, group_heads, P_SIZE, N), jnp.float32)
        block_inputs = (inner_part.reshape(blocks, CH_DEV, 1, group_heads, P_SIZE), step_sizes.reshape(blocks, CH_DEV, 1, group_heads), b_proj.reshape(blocks, CH_DEV, 1, N), c_proj.reshape(blocks, CH_DEV, 1, N))
        _, block_outs = lax.scan(one_block, start_state, block_inputs)
        ssm_out = block_outs.reshape(STRETCHES, 1, group_heads, P_SIZE) + skip_g.reshape(1, 1, group_heads, 1) * inner_part
        mixed = gated_norm(gate_part, ssm_out, gain_g)
        return (summed + jnp.dot(mixed, w_out_g, preferred_element_type=jnp.float32), None)
    group_params = (jnp.transpose(w_in.reshape(D, GROUPS, GROUP_COLS), (1, 0, 2)), jnp.transpose(w_dt.reshape(D, GROUPS, group_heads), (1, 0, 2)), pad_proj.reshape(GROUPS, GROUP_COLS), pad_dt.reshape(GROUPS, group_heads), dt_bias.reshape(GROUPS, group_heads), a_log.reshape(GROUPS, group_heads), d_skip.reshape(GROUPS, group_heads), gate_gain.reshape(GROUPS, group_heads * P_SIZE), w_out.reshape(GROUPS, group_heads * P_SIZE, D))
    summed, _ = lax.scan(one_group, jnp.zeros((STRETCHES, D), jnp.float32), group_params)
    main_out = (stretch_rows.astype(jnp.float32) + summed).astype(jnp.bfloat16)

    def smooth(state_now, pieces):
        row_value, weight = pieces
        state_next = weight * row_value + (1.0 - weight) * state_now
        return (state_next, state_next)
    _, smoothed = lax.scan(smooth, jnp.zeros((D,), jnp.float32), (main_out.astype(jnp.float32), stretch_prob.astype(jnp.float32)))
    padded = jnp.concatenate([jnp.zeros((1, D), jnp.float32), smoothed], axis=0)
    chosen_rows = jnp.take(padded, (stretch_id + 1).astype(jnp.int32), axis=0)
    return (enc_rows.astype(jnp.float32) + chosen_rows).astype(jnp.bfloat16)
```

```python
import jax
import jax.numpy as jnp
from jax import lax
from jax.sharding import Mesh
from jax.sharding import PartitionSpec as P

D = 1024
E = 2048
N = 128
HEADS_HERE = 8
P_SIZE = 64
INNER = HEADS_HERE * P_SIZE
CAP = 432
eps = 1e-05
F32 = jnp.float32
BF16 = jnp.bfloat16
highest = lax.Precision.HIGHEST


def dot(a, b, precision=None):
    return jnp.dot(a, b, preferred_element_type=F32, precision=precision)


def spread_heads(a):
    return jnp.repeat(a, P_SIZE, axis=-1)


def body(
    enc_rows,
    boundary_flags,
    boundary_prob,
    pad_vector,
    norm_gain,
    w_in,
    w_dt,
    pad_proj,
    pad_dt,
    dt_bias,
    a_log,
    d_skip,
    gate_gain,
    w_out,
):
    act = lax.axis_size("act")
    me = lax.axis_index("act")
    heads = lax.axis_size("head")
    rank = jnp.cumsum(boundary_flags)
    hit = (rank[None, :] - 1 == jnp.arange(CAP)[:, None]) & (boundary_flags > 0)[None, :]
    hit_bf = hit.astype(BF16)
    packed = dot(hit_bf, enc_rows).astype(BF16)
    prob = dot(hit_bf, boundary_prob[:, None])[:, 0]
    valid = jnp.arange(CAP) < rank[-1]

    full = lax.all_gather(packed, "head", axis=1, tiled=True)
    wide = full.astype(F32)
    energy = jnp.sum(wide * wide, axis=1) + jnp.sum(pad_vector * pad_vector)
    inverse = lax.rsqrt(energy / E + eps)
    normed = (wide * inverse[:, None] * norm_gain[None, :]).astype(BF16)
    projected = dot(normed, w_in) + inverse[:, None] * pad_proj[None, :]
    step = jax.nn.softplus(dot(normed, w_dt) + inverse[:, None] * pad_dt[None, :] + dt_bias[None, :])
    step = jnp.where(valid[:, None], step, 0.0)
    gate = projected[:, :INNER]
    x = projected[:, INNER : 2 * INNER]
    b = projected[:, 2 * INNER : 2 * INNER + N]
    c = projected[:, 2 * INNER + N :]
    running = jnp.cumsum(-jnp.exp(a_log)[None, :] * step, axis=0)
    total = running[-1]
    tail = jnp.exp(total[None, :] - running) * step
    local_state = dot(b.T, x * spread_heads(tail), highest)

    slices = local_state.reshape(act, N // act, INNER)
    logs = jnp.broadcast_to(spread_heads(total)[None, None, :], (act, 1, INNER))
    got = lax.all_to_all(jnp.concatenate([slices, logs], axis=1), "act", 0, 0)
    state = jnp.zeros_like(got[0, :-1])
    before = []
    for j in range(act):
        before.append(state)
        state = state * jnp.exp(got[j, -1])[None, :] + got[j, :-1]
    state_in = lax.all_to_all(jnp.stack(before), "act", 0, 0).reshape(N, INNER)

    lower = jnp.arange(CAP)[:, None] >= jnp.arange(CAP)[None, :]
    inter = dot(c, b.T, highest)
    outs = []
    for k in range(HEADS_HERE):
        gap = running[:, k][:, None] - running[:, k][None, :]
        w = inter * jnp.exp(jnp.where(lower, gap, -jnp.inf)) * step[:, k][None, :]
        outs.append(dot(w, x[:, k * P_SIZE : (k + 1) * P_SIZE], highest))
    ssm = jnp.concatenate(outs, axis=1)
    ssm = ssm + spread_heads(jnp.exp(running)) * dot(c, state_in.astype(F32), highest) + spread_heads(d_skip)[None, :] * x
    gated = ssm * gate / (1.0 + jnp.exp(-gate))
    power = jnp.mean(gated * gated, axis=1, keepdims=True)
    mixed = (gated * lax.rsqrt(power + eps) * gate_gain[None, :]).astype(BF16)
    partial = dot(mixed, w_out).astype(BF16)
    parts = jnp.transpose(partial.reshape(CAP, heads, -1), (1, 0, 2))
    summed = jnp.sum(lax.all_to_all(parts, "head", 0, 0).astype(F32), axis=0)
    main = (packed.astype(F32) + summed).astype(BF16)

    kept = jnp.cumsum(jnp.log1p(-prob))
    all_kept = kept[-1]
    carry = dot((prob * jnp.exp(all_kept - kept))[None, :], main.astype(F32), highest)
    sent = jnp.concatenate([carry, jnp.broadcast_to(all_kept[None, None], carry.shape)], axis=1)
    carries = lax.all_gather(sent, "act", axis=0, tiled=True)
    rows_c, logs_c = carries[:, : carry.shape[1]], carries[:, carry.shape[1]]
    earlier = jnp.arange(act) < me
    seen = jnp.where(earlier, logs_c, 0.0)
    later = jnp.cumsum(seen[::-1])[::-1] - seen
    weight = jnp.where(earlier, jnp.exp(later), 0.0)
    carry_in = jnp.sum(weight[:, None] * rows_c, axis=0)

    byte_kept = jnp.cumsum(jnp.where(boundary_flags > 0, jnp.log1p(-boundary_prob.astype(F32)), 0.0))
    covers = jnp.arange(CAP)[None, :] < rank[:, None]
    byte_gap = jnp.where(covers, byte_kept[:, None] - kept[None, :], -jnp.inf)
    w = jnp.exp(byte_gap) * prob[None, :]
    w_hi = w.astype(BF16)
    w_lo = (w - w_hi.astype(F32)).astype(BF16)
    smoothed = dot(w_hi, main) + dot(w_lo, main) + jnp.exp(byte_kept)[:, None] * carry_in[None, :]
    return (enc_rows.astype(F32) + smoothed).astype(BF16)


def solution(mesh):
    seq, heads = mesh.shape["seq"], mesh.shape["head"]
    split = Mesh(mesh.devices.reshape(2, seq // 2, heads), ("half", "act", "head"))
    seq_axes = ("half", "act")
    in_specs = (
        P(seq_axes, "head"),
        P(seq_axes),
        P(seq_axes),
        P(),
        P(),
        P(None, "head"),
        P(None, "head"),
        P("head"),
        P("head"),
        P("head"),
        P("head"),
        P("head"),
        P("head"),
        P("head", None),
    )
    return jax.shard_map(
        body, mesh=split, in_specs=in_specs, out_specs=P(seq_axes, "head"), check_vma=False
    )
```

```python
import jax
import jax.numpy as jnp
from jax import lax
from jax.experimental import pallas as pl
from jax.experimental.pallas import tpu as pltpu
from jax.sharding import Mesh
from jax.sharding import PartitionSpec as P

D = 1024
E = 2048
N = 128
HEADS_HERE = 8
P_SIZE = 64
INNER = HEADS_HERE * P_SIZE
COLS = 2 * INNER + 2 * N
CAP = 432
BYTES = 576
WIDTH = 128
CHUNKS = ((0, 128), (128, 128), (256, 128), (384, 48))
X_CHIPS = 4
LOW = -1e30
eps = 1e-05
F32 = jnp.float32
BF16 = jnp.bfloat16


def dot(a, b, contract=((1,), (0,))):
    return lax.dot_general(a, b, (contract, ((), ())), preferred_element_type=F32)


def halves(a):
    hi = a.astype(BF16)
    return hi, (a - hi.astype(F32)).astype(BF16)


def thirds(a):
    hi = a.astype(BF16)
    rest = a - hi.astype(F32)
    mid = rest.astype(BF16)
    return hi, mid, (rest - mid.astype(F32)).astype(BF16)


def dot3(a, b, contract=((1,), (0,))):
    a_hi, a_lo = halves(a)
    b_hi, b_lo = halves(b)
    return dot(a_hi, b_hi, contract) + dot(a_hi, b_lo, contract) + dot(a_lo, b_hi, contract)


def iota(shape, dim):
    return lax.broadcasted_iota(jnp.int32, shape, dim)


def spread_heads(a):
    owner = (iota((2 * HEADS_HERE, INNER), 1) // P_SIZE) == (
        iota((2 * HEADS_HERE, INNER), 0) % HEADS_HERE
    )
    hi, lo = halves(a)
    return dot(jnp.concatenate([hi, lo], axis=1), owner.astype(BF16))


def select_kernel(flags_ref, enc_ref, packed_ref):
    flags = flags_ref[...]
    upper = (iota((BYTES, BYTES), 0) <= iota((BYTES, BYTES), 1)).astype(BF16)
    rank = dot(flags.astype(F32).astype(BF16), upper)
    place = jnp.where(flags > 0, rank.astype(jnp.int32) - 1, -1)
    hit = (iota((CAP, BYTES), 0) == place).astype(F32).astype(BF16)
    packed_ref[...] = dot(hit, enc_ref[...]).astype(BF16)


def weights_kernel(flags_ref, prob_ref, w_hi_ref, w_lo_ref, carry_ref, kept_ref, decay_ref):
    flags = flags_ref[...].astype(F32)
    prob = prob_ref[...].astype(F32)
    logs = jnp.where(flags > 0, jnp.log1p(-prob), 0.0)
    before = iota((BYTES, BYTES), 1) <= iota((BYTES, BYTES), 0)
    same = iota((BYTES, BYTES), 1) == iota((BYTES, BYTES), 0)

    def column(mask, row):
        return jnp.sum(jnp.where(mask, row, 0.0), axis=1, keepdims=True)

    rank = column(before, flags)
    kept = column(before, logs)
    flag = column(same, flags)
    chance = column(same, prob)
    place = iota((BYTES, CAP), 1).astype(F32)
    hit = (place == rank - 1.0) & (flag > 0)
    kept_k = jnp.sum(jnp.where(hit, kept, 0.0), axis=0, keepdims=True)
    prob_k = jnp.sum(jnp.where(hit, chance, 0.0), axis=0, keepdims=True)
    gap = jnp.where(place < rank, kept - kept_k, LOW)
    hi, lo = halves(jnp.exp(gap) * prob_k)
    w_hi_ref[...] = hi
    w_lo_ref[...] = lo
    total = jnp.sum(logs, axis=1, keepdims=True)
    count = jnp.sum(flags, axis=1, keepdims=True)
    real = iota((1, CAP), 1).astype(F32) < count
    carry_ref[...] = jnp.exp(jnp.where(real, total - kept_k, LOW)) * prob_k
    kept_ref[...] = jnp.broadcast_to(total, (1, WIDTH))
    decay_ref[...] = jnp.exp(kept)


def project_kernel(
    r0, r1, r2, r3, s0, s1, s2, s3,
    flags_ref, pad_ref, gain_ref, w_in_ref, w_dt_ref, pad_proj_ref, pad_dt_ref, bias_ref, a_log_ref,
    proj_ref, step_ref, run_ref, run_t_ref, pieces_ref, normed_ref,
):
    x = lax.axis_index("x")
    core = lax.axis_index("core")
    blocks = (r0, r1, r2, r3, s0, s1, s2, s3)
    energy = jnp.zeros((CAP, WIDTH), F32)
    for block in blocks:
        wide = block[...].astype(F32)
        energy = energy + wide * wide
    pad = pad_ref[...]
    power = jnp.sum(energy, axis=1, keepdims=True) + jnp.sum(pad * pad)
    inverse = lax.rsqrt(power / E + eps)
    for i, block in enumerate(blocks):
        shift, other = i % X_CHIPS, i // X_CHIPS
        chip = lax.rem(x + (X_CHIPS - shift), X_CHIPS)
        owner = chip * 2 + (core if other == 0 else 1 - core)
        gain = gain_ref[pl.ds(owner, 1), :]
        lanes = pl.ds(pl.multiple_of(owner * WIDTH, WIDTH), WIDTH)
        normed_ref[:, lanes] = (block[...].astype(F32) * inverse * gain).astype(BF16)

    def tile(t, carry):
        lanes = pl.ds(pl.multiple_of(t * 256, 256), 256)
        proj_ref[:, lanes] = dot(normed_ref[...], w_in_ref[:, lanes]) + inverse * pad_proj_ref[:, lanes]
        return carry

    lax.fori_loop(0, COLS // 256, tile, 0)
    raw = dot(normed_ref[...], w_dt_ref[...]) + inverse * pad_dt_ref[...] + bias_ref[...]
    soft = jnp.maximum(raw, 0.0) + jnp.log1p(jnp.exp(-jnp.abs(raw)))
    count = jnp.sum(flags_ref[...].astype(F32), axis=1, keepdims=True)
    real = iota((CAP, HEADS_HERE), 0).astype(F32) < count
    step = jnp.where(real, soft, 0.0)
    step_ref[...] = step
    logs = -jnp.exp(a_log_ref[...]) * step
    split = jnp.concatenate(thirds(logs), axis=1)
    lower = (iota((CAP, CAP), 1) <= iota((CAP, CAP), 0)).astype(BF16)
    upper = (iota((CAP, CAP), 0) <= iota((CAP, CAP), 1)).astype(BF16)
    sums = dot(lower, split)
    h = HEADS_HERE
    run = sums[:, :h] + sums[:, h : 2 * h] + sums[:, 2 * h :]
    sums_t = dot(split, upper, ((0,), (0,)))
    run_t_ref[...] = sums_t[:h] + sums_t[h : 2 * h] + sums_t[2 * h :]
    run_ref[...] = run
    total = run[CAP - 1 :, :]
    tail = jnp.exp(total - run) * step
    weighted = proj_ref[:, INNER : 2 * INNER] * spread_heads(tail)
    state = dot3(proj_ref[:, 2 * INNER : 2 * INNER + N], weighted, ((0,), (0,)))
    total_wide = spread_heads(jnp.broadcast_to(total, (8, h)))[0:1, :]
    spare = jnp.concatenate(
        [total_wide[:, i * WIDTH : (i + 1) * WIDTH] for i in range(INNER // WIDTH)], axis=0
    )
    act = pieces_ref.shape[0]
    per = N // act
    for d in range(act):
        pieces_ref[d, :, :INNER] = state[d * per : (d + 1) * per, :]
        if per >= 4:
            pieces_ref[d, 0:4, INNER:] = spare
            if per > 4:
                pieces_ref[d, 4:, INNER:] = jnp.zeros((per - 4, WIDTH), F32)


def local_kernel(proj_ref, step_ref, run_ref, run_t_ref, skip_ref, out_ref):
    state = jnp.zeros((N, INNER), F32)
    skip = spread_heads(jnp.broadcast_to(skip_ref[...], (8, HEADS_HERE)))[0:1, :]
    start_run = jnp.zeros((1, HEADS_HERE), F32)
    for start, length in CHUNKS:
        rows = slice(start, start + length)
        x = proj_ref[rows, INNER : 2 * INNER]
        b = proj_ref[rows, 2 * INNER : 2 * INNER + N]
        c = proj_ref[rows, 2 * INNER + N :]
        run = run_ref[rows, :]
        step = step_ref[rows, :]
        end_run = run[length - 1 :, :]
        scaled = (x * spread_heads(step)).astype(BF16)
        inter = dot3(c, b, ((1,), (1,)))
        lower = iota((length, length), 0) >= iota((length, length), 1)
        outs = []
        for k in range(HEADS_HERE):
            gap = run[:, k : k + 1] - run_t_ref[k : k + 1, rows]
            w = inter * jnp.exp(jnp.where(lower, gap, LOW))
            outs.append(dot(w.astype(BF16), scaled[:, k * P_SIZE : (k + 1) * P_SIZE]))
        y = jnp.concatenate(outs, axis=1) + skip * x
        if start > 0:
            y = y + spread_heads(jnp.exp(run - start_run)) * dot3(c, state)
        out_ref[rows, :] = y
        if start + length < CAP:
            weighted = x * spread_heads(step * jnp.exp(end_run - run))
            kept = spread_heads(jnp.broadcast_to(jnp.exp(end_run - start_run), (8, HEADS_HERE)))
            state = state * kept[0:1, :] + dot3(b, weighted, ((0,), (0,)))
        start_run = end_run


def scan_kernel(got_ref, before_ref):
    act, per, _ = got_ref.shape
    state = jnp.zeros((per, INNER), F32)
    for j in range(act):
        before_ref[j] = state
        keep = jnp.exp(got_ref[j, 0:4, INNER:])
        keep = jnp.concatenate([keep[i : i + 1, :] for i in range(INNER // WIDTH)], axis=1)
        state = state * keep + got_ref[j, :, :INNER]


def output_kernel(proj_ref, run_ref, local_ref, state_ref, gain_ref, w_out_ref, kept_ref, sent_ref, full_ref):
    core = lax.axis_index("core")
    act, per, _ = state_ref.shape
    for d in range(act):
        full_ref[d * per : (d + 1) * per, :] = state_ref[d]
    c = proj_ref[:, 2 * INNER + N :]
    ssm = local_ref[...] + spread_heads(jnp.exp(run_ref[...])) * dot3(c, full_ref[...])
    gate = proj_ref[:, :INNER]
    gated = ssm * gate / (1.0 + jnp.exp(-gate))
    power = jnp.mean(gated * gated, axis=1, keepdims=True)
    mixed = (gated * lax.rsqrt(power + eps) * gain_ref[...]).astype(BF16)
    for i in range(X_CHIPS):
        pair = dot(mixed, w_out_ref[:, i * 2 * WIDTH : (i + 1) * 2 * WIDTH])
        first, second = pair[:, :WIDTH], pair[:, WIDTH:]
        kept_ref[i] = jnp.where(core == 0, first, second)
        sent_ref[i] = jnp.where(core == 0, second, first).astype(BF16)


def main_kernel(packed_ref, parts_ref, carry_ref, kept_ref, main_ref, sent_ref):
    summed = packed_ref[...].astype(F32)
    added = parts_ref[0].astype(F32)
    for i in range(1, X_CHIPS):
        added = added + parts_ref[i].astype(F32)
    main = (summed + added).astype(BF16)
    main_ref[...] = main
    split = jnp.concatenate([jnp.broadcast_to(p, (8, CAP)) for p in thirds(carry_ref[...])], axis=0)
    sums = dot(split, main)
    carry = sums[0:1] + sums[8:9] + sums[16:17]
    row = jnp.concatenate([carry, kept_ref[...]], axis=0)
    sent_ref[...] = jnp.broadcast_to(row[None], sent_ref.shape)


def decode_kernel(enc_ref, w_hi_ref, w_lo_ref, main_ref, decay_ref, carries_ref, out_ref):
    me = lax.axis_index("act")
    act = carries_ref.shape[0]
    carry = jnp.zeros((1, WIDTH), F32)
    for j in range(act):
        after = carry * jnp.exp(carries_ref[j, 1:2, :]) + carries_ref[j, 0:1, :]
        carry = jnp.where(j < me, after, carry)
    main = main_ref[...]
    smoothed = dot(w_hi_ref[...], main) + dot(w_lo_ref[...], main) + decay_ref[...] * carry
    out_ref[...] = (enc_ref[...].astype(F32) + smoothed).astype(BF16)


def shape(dims, dtype=F32):
    return jax.ShapeDtypeStruct(dims, dtype)


def call(kernel, outs, name, scratch=(), flops=0, transcendentals=0, nbytes=0):
    return pl.pallas_call(
        kernel,
        out_shape=outs,
        name=name,
        scratch_shapes=scratch,
        compiler_params=pltpu.CompilerParams(vmem_limit_bytes=40 * 2**20),
        cost_estimate=pl.CostEstimate(
            flops=flops, transcendentals=transcendentals, bytes_accessed=nbytes
        ),
    )


def body(
    enc_rows,
    boundary_flags,
    boundary_prob,
    pad_vector,
    norm_gain,
    w_in,
    w_dt,
    pad_proj,
    pad_dt,
    dt_bias,
    a_log,
    d_skip,
    gate_gain,
    w_out,
):
    act = lax.axis_size("act")
    row = lambda a: a.reshape(1, -1)
    flags, prob = row(boundary_flags), row(boundary_prob)
    packed = call(select_kernel, shape((CAP, WIDTH), BF16), "select", flops=10**8)(flags, enc_rows)

    around = [packed] + [
        lax.ppermute(packed, "x", [(i, (i + s) % X_CHIPS) for i in range(X_CHIPS)])
        for s in range(1, X_CHIPS)
    ]
    across = [lax.ppermute(a, "core", [(0, 1), (1, 0)]) for a in around]

    w_hi, w_lo, carry_w, kept, decay = call(
        weights_kernel,
        (
            shape((BYTES, CAP), BF16),
            shape((BYTES, CAP), BF16),
            shape((1, CAP)),
            shape((1, WIDTH)),
            shape((BYTES, 1)),
        ),
        "weights",
        transcendentals=BYTES * CAP,
        flops=BYTES * CAP * 30,
        nbytes=10**6,
    )(flags, prob)

    proj, step, run, run_t, pieces = call(
        project_kernel,
        (
            shape((CAP, COLS)),
            shape((CAP, HEADS_HERE)),
            shape((CAP, HEADS_HERE)),
            shape((HEADS_HERE, CAP)),
            shape((act, N // act, INNER + WIDTH)),
        ),
        "project",
        scratch=[pltpu.VMEM((CAP, D), BF16)],
        flops=2 * CAP * D * COLS,
        nbytes=8 * 10**6,
    )(
        *around, *across, flags, pad_vector.reshape(-1, WIDTH), norm_gain.reshape(-1, WIDTH), w_in, w_dt,
        row(pad_proj), row(pad_dt), row(dt_bias), row(a_log),
    )

    got = lax.all_to_all(pieces, "act", 0, 0)
    local = call(
        local_kernel, shape((CAP, INNER)), "local", flops=10**9, transcendentals=CAP * 1024, nbytes=3 * 10**6
    )(proj, step, run, run_t, row(d_skip))
    before = call(scan_kernel, shape((act, N // act, INNER)), "scan", nbytes=6 * 10**5)(got)
    state_in = lax.all_to_all(before, "act", 0, 0)

    own, sent = call(
        output_kernel,
        (shape((X_CHIPS, CAP, WIDTH)), shape((X_CHIPS, CAP, WIDTH), BF16)),
        "output",
        scratch=[pltpu.VMEM((N, INNER), F32)],
        flops=2 * CAP * INNER * D,
        nbytes=6 * 10**6,
    )(proj, run, local, state_in, row(gate_gain), w_out)

    pair = (own + lax.ppermute(sent, "core", [(0, 1), (1, 0)]).astype(F32)).astype(BF16)
    parts = lax.all_to_all(pair, "x", 0, 0)
    main, carry = call(
        main_kernel, (shape((CAP, WIDTH), BF16), shape((act, 2, WIDTH))), "main", nbytes=6 * 10**5
    )(packed, parts, carry_w, kept)
    carries = lax.all_to_all(carry, "act", 0, 0)
    return call(
        decode_kernel, shape((BYTES, WIDTH), BF16), "decode", flops=2 * 10**8, nbytes=2 * 10**6
    )(enc_rows, w_hi, w_lo, main, decay, carries)


def solution(mesh):
    seq = mesh.shape["seq"]
    split = Mesh(
        mesh.devices.reshape(2, seq // 2, X_CHIPS, 2), ("half", "act", "x", "core")
    )
    by_seq, by_head = ("half", "act"), ("x", "core")
    in_specs = (
        P(by_seq, by_head),
        P(by_seq),
        P(by_seq),
        P(),
        P(),
        P(None, by_head),
        P(None, by_head),
        P(by_head),
        P(by_head),
        P(by_head),
        P(by_head),
        P(by_head),
        P(by_head),
        P(by_head, None),
    )
    return jax.shard_map(
        body, mesh=split, in_specs=in_specs, out_specs=P(by_seq, by_head), check_vma=False
    )
```

```python
import jax
import jax.numpy as jnp
from jax import lax
from jax.experimental import pallas as pl
from jax.experimental.pallas import tpu as pltpu
from jax.sharding import Mesh
from jax.sharding import PartitionSpec as P

D = 1024
E = 2048
N = 128
HEADS_HERE = 8
P_SIZE = 64
INNER = HEADS_HERE * P_SIZE
COLS = 2 * INNER + 2 * N
CAP = 432
BYTES = 576
WIDTH = 128
CHUNKS = ((0, 128), (128, 128), (256, 128), (384, 48))
X_CHIPS = 4
Z_CHIPS = 8
LOW = -1e30
eps = 1e-05
F32 = jnp.float32
BF16 = jnp.bfloat16


def dot(a, b, contract=((1,), (0,))):
    return lax.dot_general(a, b, (contract, ((), ())), preferred_element_type=F32)


def halves(a):
    hi = a.astype(BF16)
    return hi, (a - hi.astype(F32)).astype(BF16)


def thirds(a):
    hi = a.astype(BF16)
    rest = a - hi.astype(F32)
    mid = rest.astype(BF16)
    return hi, mid, (rest - mid.astype(F32)).astype(BF16)


def dot3(a, b, contract=((1,), (0,))):
    a_hi, a_lo = halves(a)
    b_hi, b_lo = halves(b)
    return dot(a_hi, b_hi, contract) + dot(a_hi, b_lo, contract) + dot(a_lo, b_hi, contract)


def iota(shape, dim):
    return lax.broadcasted_iota(jnp.int32, shape, dim)


def spread_heads(a):
    owner = (iota((2 * HEADS_HERE, INNER), 1) // P_SIZE) == (
        iota((2 * HEADS_HERE, INNER), 0) % HEADS_HERE
    )
    hi, lo = halves(a)
    return dot(jnp.concatenate([hi, lo], axis=1), owner.astype(BF16))


def select_kernel(flags_ref, enc_ref, packed_ref):
    flags = flags_ref[...]
    upper = (iota((BYTES, BYTES), 0) <= iota((BYTES, BYTES), 1)).astype(BF16)
    rank = dot(flags.astype(F32).astype(BF16), upper)
    place = jnp.where(flags > 0, rank.astype(jnp.int32) - 1, -1)
    hit = (iota((CAP, BYTES), 0) == place).astype(F32).astype(BF16)
    packed_ref[...] = dot(hit, enc_ref[...]).astype(BF16)


def weights_kernel(*refs):
    flags_ref, prob_ref = refs[:2]
    staged = (len(refs) - 8) // 2
    given, (w_hi_ref, w_lo_ref, carry_ref, kept_ref, decay_ref) = refs[2 : 2 + staged], refs[2 + staged : 7 + staged]
    held, sems = refs[7 + staged : 7 + 2 * staged], refs[-1]
    copies = [pltpu.make_async_copy(a, b, sems.at[i]) for i, (a, b) in enumerate(zip(given, held))]
    for copy in copies:
        copy.start()
    flags = flags_ref[...].astype(F32)
    prob = prob_ref[...].astype(F32)
    logs = jnp.where(flags > 0, jnp.log1p(-prob), 0.0)
    before = iota((BYTES, BYTES), 1) <= iota((BYTES, BYTES), 0)
    same = iota((BYTES, BYTES), 1) == iota((BYTES, BYTES), 0)

    def column(mask, row):
        return jnp.sum(jnp.where(mask, row, 0.0), axis=1, keepdims=True)

    rank = column(before, flags)
    kept = column(before, logs)
    flag = column(same, flags)
    chance = column(same, prob)
    place = iota((BYTES, CAP), 1).astype(F32)
    hit = (place == rank - 1.0) & (flag > 0)
    kept_k = jnp.sum(jnp.where(hit, kept, 0.0), axis=0, keepdims=True)
    prob_k = jnp.sum(jnp.where(hit, chance, 0.0), axis=0, keepdims=True)
    gap = jnp.where(place < rank, kept - kept_k, LOW)
    hi, lo = halves(jnp.exp(gap) * prob_k)
    w_hi_ref[...] = hi
    w_lo_ref[...] = lo
    total = jnp.sum(logs, axis=1, keepdims=True)
    count = jnp.sum(flags, axis=1, keepdims=True)
    real = iota((1, CAP), 1).astype(F32) < count
    carry_ref[...] = jnp.exp(jnp.where(real, total - kept_k, LOW)) * prob_k
    kept_ref[...] = jnp.broadcast_to(total, (1, WIDTH))
    decay_ref[...] = jnp.exp(kept)
    for copy in copies:
        copy.wait()


def stack_kernel(r0, r1, r2, r3, out_ref):
    for i, block in enumerate((r0, r1, r2, r3)):
        out_ref[i] = block[...]


def project_kernel(
    near_ref, far_ref, flags_ref, pad_ref, gain_ref, w_in_ref, w_dt_ref, pad_proj_ref, pad_dt_ref, bias_ref, a_log_ref,
    proj_ref, step_ref, run_ref, run_t_ref, pieces_ref, normed_ref,
):
    x = lax.axis_index("x")
    core = lax.axis_index("core")
    blocks = [ref[i] for ref in (near_ref, far_ref) for i in range(X_CHIPS)]
    energy = jnp.zeros((CAP, WIDTH), F32)
    for block in blocks:
        wide = block.astype(F32)
        energy = energy + wide * wide
    pad = pad_ref[...]
    power = jnp.sum(energy, axis=1, keepdims=True) + jnp.sum(pad * pad)
    inverse = lax.rsqrt(power / E + eps)
    for i, block in enumerate(blocks):
        shift, other = i % X_CHIPS, i // X_CHIPS
        chip = lax.rem(x + (X_CHIPS - shift), X_CHIPS)
        owner = chip * 2 + (core if other == 0 else 1 - core)
        gain = gain_ref[pl.ds(owner, 1), :]
        lanes = pl.ds(pl.multiple_of(owner * WIDTH, WIDTH), WIDTH)
        normed_ref[:, lanes] = (block.astype(F32) * inverse * gain).astype(BF16)

    def tile(t, carry):
        lanes = pl.ds(pl.multiple_of(t * 256, 256), 256)
        proj_ref[:, lanes] = dot(normed_ref[...], w_in_ref[:, lanes]) + inverse * pad_proj_ref[:, lanes]
        return carry

    lax.fori_loop(0, COLS // 256, tile, 0)
    raw = dot(normed_ref[...], w_dt_ref[...], ((1,), (1,))) + inverse * pad_dt_ref[...] + bias_ref[...]
    soft = jnp.maximum(raw, 0.0) + jnp.log1p(jnp.exp(-jnp.abs(raw)))
    count = jnp.sum(flags_ref[...].astype(F32), axis=1, keepdims=True)
    real = iota((CAP, HEADS_HERE), 0).astype(F32) < count
    step = jnp.where(real, soft, 0.0)
    step_ref[...] = step
    logs = -jnp.exp(a_log_ref[...]) * step
    split = jnp.concatenate(thirds(logs), axis=1)
    lower = (iota((CAP, CAP), 1) <= iota((CAP, CAP), 0)).astype(BF16)
    upper = (iota((CAP, CAP), 0) <= iota((CAP, CAP), 1)).astype(BF16)
    sums = dot(lower, split)
    h = HEADS_HERE
    run = sums[:, :h] + sums[:, h : 2 * h] + sums[:, 2 * h :]
    sums_t = dot(split, upper, ((0,), (0,)))
    run_t_ref[...] = sums_t[:h] + sums_t[h : 2 * h] + sums_t[2 * h :]
    run_ref[...] = run
    total = run[CAP - 1 :, :]
    tail = jnp.exp(total - run) * step
    weighted = proj_ref[:, INNER : 2 * INNER] * spread_heads(tail)
    state = dot3(proj_ref[:, 2 * INNER : 2 * INNER + N], weighted, ((0,), (0,)))
    total_wide = spread_heads(jnp.broadcast_to(total, (8, h)))[0:1, :]
    spare = jnp.concatenate(
        [total_wide[:, i * WIDTH : (i + 1) * WIDTH] for i in range(INNER // WIDTH)], axis=0
    )
    parts = pieces_ref.shape[0]
    per = N // parts
    for d in range(parts):
        pieces_ref[d, :, :INNER] = state[d * per : (d + 1) * per, :]
        pieces_ref[d, 0:4, INNER:] = spare
        pieces_ref[d, 4:, INNER:] = jnp.zeros((per - 4, WIDTH), F32)


def local_kernel(proj_ref, step_ref, run_ref, run_t_ref, skip_ref, out_ref):
    state = jnp.zeros((N, INNER), F32)
    skip = spread_heads(jnp.broadcast_to(skip_ref[...], (8, HEADS_HERE)))[0:1, :]
    start_run = jnp.zeros((1, HEADS_HERE), F32)
    for start, length in CHUNKS:
        rows = slice(start, start + length)
        x = proj_ref[rows, INNER : 2 * INNER]
        b = proj_ref[rows, 2 * INNER : 2 * INNER + N]
        c = proj_ref[rows, 2 * INNER + N :]
        run = run_ref[rows, :]
        step = step_ref[rows, :]
        end_run = run[length - 1 :, :]
        scaled = (x * spread_heads(step)).astype(BF16)
        inter = dot3(c, b, ((1,), (1,)))
        lower = iota((length, length), 0) >= iota((length, length), 1)
        outs = []
        for k in range(HEADS_HERE):
            gap = run[:, k : k + 1] - run_t_ref[k : k + 1, rows]
            w = inter * jnp.exp(jnp.where(lower, gap, LOW))
            outs.append(dot(w.astype(BF16), scaled[:, k * P_SIZE : (k + 1) * P_SIZE]))
        y = jnp.concatenate(outs, axis=1) + skip * x
        if start > 0:
            y = y + spread_heads(jnp.exp(run - start_run)) * dot3(c, state)
        out_ref[rows, :] = y
        if start + length < CAP:
            weighted = x * spread_heads(step * jnp.exp(end_run - run))
            kept = spread_heads(jnp.broadcast_to(jnp.exp(end_run - start_run), (8, HEADS_HERE)))
            state = state * kept[0:1, :] + dot3(b, weighted, ((0,), (0,)))
        start_run = end_run


def keep_of(logs):
    keep = jnp.exp(logs)
    return jnp.concatenate([keep[i : i + 1, :] for i in range(INNER // WIDTH)], axis=1)


def total_kernel(got_ref, total_ref):
    state, logs = got_ref[0, :, :INNER], got_ref[0, :, INNER:]
    for j in range(1, got_ref.shape[0]):
        more = got_ref[j, :, INNER:]
        state = state * keep_of(more[0:4]) + got_ref[j, :, :INNER]
        logs = logs + more
    for i in range(total_ref.shape[0]):
        total_ref[i, :, :INNER] = state
        total_ref[i, :, INNER:] = logs


def scan_kernel(got_ref, rows_ref, before_ref):
    y = lax.axis_index("y")
    state = jnp.zeros(before_ref.shape[1:], F32)
    for j in range(rows_ref.shape[0]):
        after = state * keep_of(rows_ref[j, 0:4, INNER:]) + rows_ref[j, :, :INNER]
        state = jnp.where(j < y, after, state)
    for j in range(got_ref.shape[0]):
        before_ref[j] = state
        state = state * keep_of(got_ref[j, 0:4, INNER:]) + got_ref[j, :, :INNER]


def output_kernel(proj_ref, run_ref, local_ref, state_ref, gain_ref, w_out_ref, kept_ref, sent_ref, full_ref):
    core = lax.axis_index("core")
    act, per, _ = state_ref.shape
    for d in range(act):
        full_ref[d * per : (d + 1) * per, :] = state_ref[d]
    c = proj_ref[:, 2 * INNER + N :]
    ssm = local_ref[...] + spread_heads(jnp.exp(run_ref[...])) * dot3(c, full_ref[...])
    gate = proj_ref[:, :INNER]
    gated = ssm * gate / (1.0 + jnp.exp(-gate))
    power = jnp.mean(gated * gated, axis=1, keepdims=True)
    mixed = (gated * lax.rsqrt(power + eps) * gain_ref[...]).astype(BF16)
    for i in range(X_CHIPS):
        pair = dot(mixed, w_out_ref[:, i * 2 * WIDTH : (i + 1) * 2 * WIDTH])
        first, second = pair[:, :WIDTH], pair[:, WIDTH:]
        kept_ref[i] = jnp.where(core == 0, first, second)
        sent_ref[i] = jnp.where(core == 0, second, first).astype(BF16)


def pair_kernel(packed_ref, own_ref, got_ref, keep_ref, s1, s2, s3):
    x = lax.axis_index("x")
    keep_ref[...] = packed_ref[...].astype(F32) + (own_ref[x] + got_ref[x].astype(F32))
    for s, out_ref in enumerate((s1, s2, s3), start=1):
        chip = lax.rem(x + s, X_CHIPS)
        out_ref[...] = (own_ref[chip] + got_ref[chip].astype(F32)).astype(BF16)


def main_kernel(keep_ref, r1, r2, r3, carry_ref, kept_ref, main_ref, sent_ref):
    added = r1[...].astype(F32) + r2[...].astype(F32) + r3[...].astype(F32)
    main = (keep_ref[...] + added).astype(BF16)
    main_ref[...] = main
    split = jnp.concatenate([jnp.broadcast_to(p, (8, CAP)) for p in thirds(carry_ref[...])], axis=0)
    sums = dot(split, main)
    carry = sums[0:1] + sums[8:9] + sums[16:17]
    row = jnp.concatenate([carry, kept_ref[...]], axis=0)
    sent_ref[...] = jnp.broadcast_to(row[None], sent_ref.shape)


def carry_kernel(got_ref, sent_ref):
    carry, logs = got_ref[0, 0:1, :], got_ref[0, 1:2, :]
    for j in range(1, got_ref.shape[0]):
        more = got_ref[j, 1:2, :]
        carry = carry * jnp.exp(more) + got_ref[j, 0:1, :]
        logs = logs + more
    row = jnp.concatenate([carry, logs], axis=0)
    sent_ref[...] = jnp.broadcast_to(row[None], sent_ref.shape)


def decode_kernel(enc_ref, w_hi_ref, w_lo_ref, main_ref, decay_ref, row_ref, rows_ref, out_ref):
    carry = jnp.zeros((1, WIDTH), F32)
    for ref, place in ((rows_ref, lax.axis_index("y")), (row_ref, lax.axis_index("z"))):
        for j in range(ref.shape[0]):
            after = carry * jnp.exp(ref[j, 1:2, :]) + ref[j, 0:1, :]
            carry = jnp.where(j < place, after, carry)
    main = main_ref[...]
    smoothed = dot(w_hi_ref[...], main) + dot(w_lo_ref[...], main) + decay_ref[...] * carry
    out_ref[...] = (enc_ref[...].astype(F32) + smoothed).astype(BF16)


def shape(dims, dtype=F32):
    return jax.ShapeDtypeStruct(dims, dtype)


def call(kernel, outs, name, in_specs=None, scratch=(), vmem=12, flops=0, transcendentals=0, nbytes=0):
    more = {} if in_specs is None else {"in_specs": in_specs}
    return pl.pallas_call(
        kernel,
        out_shape=outs,
        name=name,
        scratch_shapes=scratch,
        compiler_params=pltpu.CompilerParams(vmem_limit_bytes=vmem * 2**20),
        cost_estimate=pl.CostEstimate(
            flops=flops, transcendentals=transcendentals, bytes_accessed=nbytes
        ),
        **more,
    )


def over_chips(a, s):
    return lax.ppermute(a, "x", [(i, (i + s) % X_CHIPS) for i in range(X_CHIPS)])


def body(
    enc_rows,
    boundary_flags,
    boundary_prob,
    pad_vector,
    norm_gain,
    w_in,
    w_dt,
    pad_proj,
    pad_dt,
    dt_bias,
    a_log,
    d_skip,
    gate_gain,
    w_out,
):
    y_size, z_size = lax.axis_size("y"), lax.axis_size("z")
    row = lambda a: a.reshape(1, -1)
    flags, prob = row(boundary_flags), row(boundary_prob)
    packed = call(select_kernel, shape((CAP, WIDTH), BF16), "select", flops=10**8)(flags, enc_rows)

    around = [over_chips(packed, s) for s in range(1, X_CHIPS)]
    near = call(stack_kernel, shape((X_CHIPS, CAP, WIDTH), BF16), "stack", nbytes=10**6)(packed, *around)
    far = lax.ppermute(near, "core", [(0, 1), (1, 0)])

    given = [
        w_in, w_out, w_dt.T, pad_vector.reshape(-1, WIDTH), norm_gain.reshape(-1, WIDTH), row(pad_proj),
        row(pad_dt), row(dt_bias), row(a_log), row(d_skip), row(gate_gain),
    ]
    any_spec, vmem_spec = pl.BlockSpec(memory_space=pl.ANY), pl.BlockSpec(memory_space=pltpu.VMEM)
    w_hi, w_lo, carry_w, kept, decay, *held = call(
        weights_kernel,
        [
            shape((BYTES, CAP), BF16),
            shape((BYTES, CAP), BF16),
            shape((1, CAP)),
            shape((1, WIDTH)),
            shape((BYTES, 1)),
        ]
        + [shape(a.shape, a.dtype) for a in given],
        "weights",
        in_specs=[vmem_spec] * 2 + [any_spec] * len(given),
        scratch=[pltpu.SemaphoreType.DMA((len(given),))],
        vmem=16,
        transcendentals=BYTES * CAP,
        flops=BYTES * CAP * 30,
        nbytes=5 * 10**6,
    )(flags, prob, *given)
    w_in, w_out, w_dt, pad_vector, norm_gain, pad_proj, pad_dt, dt_bias, a_log, d_skip, gate_gain = held

    proj, step, run, run_t, pieces = call(
        project_kernel,
        (
            shape((CAP, COLS)),
            shape((CAP, HEADS_HERE)),
            shape((CAP, HEADS_HERE)),
            shape((HEADS_HERE, CAP)),
            shape((z_size, N // z_size, INNER + WIDTH)),
        ),
        "project",
        scratch=[pltpu.VMEM((CAP, D), BF16)],
        vmem=20,
        flops=2 * CAP * D * COLS,
        nbytes=8 * 10**6,
    )(near, far, flags, pad_vector, norm_gain, w_in, w_dt, pad_proj, pad_dt, dt_bias, a_log)

    got = lax.all_to_all(pieces, "z", 0, 0)
    totals = call(total_kernel, shape((y_size,) + pieces.shape[1:]), "total", nbytes=4 * 10**5)(got)
    rows = lax.all_to_all(totals, "y", 0, 0)
    local = call(
        local_kernel, shape((CAP, INNER)), "local", flops=10**9, transcendentals=CAP * 1024, nbytes=3 * 10**6
    )(proj, step, run, run_t, d_skip)
    before = call(scan_kernel, shape((z_size, N // z_size, INNER)), "scan", nbytes=6 * 10**5)(got, rows)
    state_in = lax.all_to_all(before, "z", 0, 0)

    own, sent = call(
        output_kernel,
        (shape((X_CHIPS, CAP, WIDTH)), shape((X_CHIPS, CAP, WIDTH), BF16)),
        "output",
        scratch=[pltpu.VMEM((N, INNER), F32)],
        vmem=16,
        flops=2 * CAP * INNER * D,
        nbytes=6 * 10**6,
    )(proj, run, local, state_in, gate_gain, w_out)

    got_sums = lax.ppermute(sent, "core", [(0, 1), (1, 0)])
    block = shape((CAP, WIDTH), BF16)
    keep, *parts = call(
        pair_kernel, (shape((CAP, WIDTH)), block, block, block), "pair", nbytes=2 * 10**6
    )(packed, own, got_sums)
    parts = [over_chips(a, s) for s, a in enumerate(parts, start=1)]
    main, carry = call(
        main_kernel, (block, shape((z_size, 2, WIDTH))), "main", nbytes=6 * 10**5
    )(keep, *parts, carry_w, kept)
    row_carries = lax.all_to_all(carry, "z", 0, 0)
    row_total = call(carry_kernel, shape((y_size, 2, WIDTH)), "carry")(row_carries)
    all_carries = lax.all_to_all(row_total, "y", 0, 0)
    return call(
        decode_kernel, shape((BYTES, WIDTH), BF16), "decode", flops=2 * 10**8, nbytes=2 * 10**6
    )(enc_rows, w_hi, w_lo, main, decay, row_carries, all_carries)


def solution(mesh):
    seq = mesh.shape["seq"]
    split = Mesh(
        mesh.devices.reshape(2, seq // 2 // Z_CHIPS, Z_CHIPS, X_CHIPS, 2),
        ("half", "y", "z", "x", "core"),
    )
    by_seq, by_head = ("half", "y", "z"), ("x", "core")
    in_specs = (
        P(by_seq, by_head),
        P(by_seq),
        P(by_seq),
        P(),
        P(),
        P(None, by_head),
        P(None, by_head),
        P(by_head),
        P(by_head),
        P(by_head),
        P(by_head),
        P(by_head),
        P(by_head),
        P(by_head, None),
    )
    return jax.shard_map(
        body, mesh=split, in_specs=in_specs, out_specs=P(by_seq, by_head), check_vma=False
    )
```

```python
import jax
import jax.numpy as jnp
from jax import lax
from jax.experimental import pallas as pl
from jax.experimental.pallas import tpu as pltpu
from jax.sharding import Mesh
from jax.sharding import PartitionSpec as P

D = 1024
E = 2048
N = 128
HEADS_HERE = 8
P_SIZE = 64
INNER = HEADS_HERE * P_SIZE
COLS = 2 * INNER + 2 * N
CAP = 432
HEAD_PARTS = 8
BYTES = 576
WIDTH = 128
CHUNKS = ((0, 128), (128, 128), (256, 128), (384, 48))
LOW = -1e30
XBC = INNER + 2 * N
VMEM_LIMIT = 60 * 2**20
eps = 1e-05
F32 = jnp.float32
BF16 = jnp.bfloat16


def dot(a, b, contract=((1,), (0,))):
    return lax.dot_general(a, b, (contract, ((), ())), preferred_element_type=F32)


def halves(a):
    hi = a.astype(BF16)
    return hi, (a - hi.astype(F32)).astype(BF16)


def thirds(a):
    hi = a.astype(BF16)
    rest = a - hi.astype(F32)
    mid = rest.astype(BF16)
    return hi, mid, (rest - mid.astype(F32)).astype(BF16)


def dot3(a, b, contract=((1,), (0,))):
    a_hi, a_lo = halves(a)
    b_hi, b_lo = halves(b)
    return dot(a_hi, b_hi, contract) + dot(a_hi, b_lo, contract) + dot(a_lo, b_hi, contract)


def iota(shape, dim):
    return lax.broadcasted_iota(jnp.int32, shape, dim)


def spread_heads(a):
    owner = (iota((2 * HEADS_HERE, INNER), 1) // P_SIZE) == (
        iota((2 * HEADS_HERE, INNER), 0) % HEADS_HERE
    )
    hi, lo = halves(a)
    return dot(jnp.concatenate([hi, lo], axis=1), owner.astype(BF16))


def line(ref):
    return ref[...].reshape(1, ref.shape[0])


def select_kernel(flags_ref, enc_ref, packed_ref):
    flags = line(flags_ref)
    upper = (iota((BYTES, BYTES), 0) <= iota((BYTES, BYTES), 1)).astype(BF16)
    rank = dot(flags.astype(F32).astype(BF16), upper)
    place = jnp.where(flags > 0, rank.astype(jnp.int32) - 1, -1)
    hit = (iota((CAP, BYTES), 0) == place).astype(F32).astype(BF16)
    packed_ref[...] = dot(hit, enc_ref[...]).astype(BF16)


def weights_kernel(flags_ref, prob_ref, w_hi_ref, w_lo_ref, carry_ref, kept_ref, decay_ref):
    flags = line(flags_ref).astype(F32)
    prob = prob_ref[...].astype(F32).reshape(1, BYTES)
    logs = jnp.where(flags > 0, jnp.log1p(-prob), 0.0)
    before = iota((BYTES, BYTES), 1) <= iota((BYTES, BYTES), 0)
    same = iota((BYTES, BYTES), 1) == iota((BYTES, BYTES), 0)

    def column(mask, row):
        return jnp.sum(jnp.where(mask, row, 0.0), axis=1, keepdims=True)

    rank = column(before, flags)
    kept = column(before, logs)
    flag = column(same, flags)
    chance = column(same, prob)
    place = iota((BYTES, CAP), 1).astype(F32)
    hit = (place == rank - 1.0) & (flag > 0)
    kept_k = jnp.sum(jnp.where(hit, kept, 0.0), axis=0, keepdims=True)
    prob_k = jnp.sum(jnp.where(hit, chance, 0.0), axis=0, keepdims=True)
    gap = jnp.where(place < rank, kept - kept_k, LOW)
    hi, lo = halves(jnp.exp(gap) * prob_k)
    w_hi_ref[...] = hi
    w_lo_ref[...] = lo
    total = jnp.sum(logs, axis=1, keepdims=True)
    count = jnp.sum(flags, axis=1, keepdims=True)
    real = iota((1, CAP), 1).astype(F32) < count
    carry_ref[...] = jnp.exp(jnp.where(real, total - kept_k, LOW)) * prob_k
    kept_ref[...] = jnp.broadcast_to(total, (1, WIDTH))
    decay_ref[...] = jnp.exp(kept)


def log_decays(step, a_log_ref):
    return -jnp.exp(line(a_log_ref)) * step


def sum_thirds(sums, axis):
    h = HEADS_HERE
    if axis == 0:
        return sums[:h] + sums[h : 2 * h] + sums[2 * h :]
    return sums[:, :h] + sums[:, h : 2 * h] + sums[:, 2 * h :]


def project_kernel(
    rows_ref, flags_ref, pad_ref, gain_ref, w_in_ref, w_dt_ref, pad_proj_ref, pad_dt_ref, bias_ref, a_log_ref,
    xbc_ref, normed_ref, inverse_ref, step_ref, run_ref, pieces_ref, w_ref, sems,
):
    tiles = range(XBC // 256)
    copies = [
        pltpu.make_async_copy(
            w_in_ref.at[:, INNER + 256 * t : INNER + 256 * (t + 1)], w_ref.at[t], sems.at[t]
        )
        for t in tiles
    ]
    for copy in copies:
        copy.start()
    energy = jnp.zeros((CAP, WIDTH), F32)
    for i in range(HEAD_PARTS):
        wide = rows_ref[:, i * WIDTH : (i + 1) * WIDTH].astype(F32)
        energy = energy + wide * wide
    pad = line(pad_ref)
    power = jnp.sum(energy, axis=1, keepdims=True) + jnp.sum(pad * pad)
    inverse = lax.rsqrt(power / E + eps)
    inverse_ref[...] = inverse
    gain = line(gain_ref)
    for i in range(HEAD_PARTS):
        lanes = slice(i * WIDTH, (i + 1) * WIDTH)
        normed_ref[:, lanes] = (rows_ref[:, lanes].astype(F32) * inverse * gain[:, lanes]).astype(BF16)
    h = HEADS_HERE
    raw = dot(normed_ref[...], w_dt_ref[...], ((1,), (1,))) + inverse * line(pad_dt_ref) + line(bias_ref)
    soft = jnp.maximum(raw, 0.0) + jnp.log1p(jnp.exp(-jnp.abs(raw)))
    count = jnp.sum(line(flags_ref).astype(F32), axis=1, keepdims=True)
    step = jnp.where(iota((CAP, h), 0).astype(F32) < count, soft, 0.0)
    step_ref[...] = step
    split = jnp.concatenate(thirds(log_decays(step, a_log_ref)), axis=1)
    lower = (iota((CAP, CAP), 1) <= iota((CAP, CAP), 0)).astype(BF16)
    run = sum_thirds(dot(lower, split), 1)
    run_ref[...] = run
    total = run[CAP - 1 :, :]
    tail = spread_heads(jnp.exp(total - run) * step)
    pad_proj = line(pad_proj_ref)
    for t in tiles:
        copies[t].wait()
        lanes = slice(256 * t, 256 * (t + 1))
        offset = inverse * pad_proj[:, INNER + 256 * t : INNER + 256 * (t + 1)]
        xbc_ref[:, lanes] = dot(normed_ref[...], w_ref[t]) + offset
    state = dot3(xbc_ref[:, INNER : INNER + N], xbc_ref[:, :INNER] * tail, ((0,), (0,)))
    total_wide = spread_heads(jnp.broadcast_to(total, (8, h)))[0:1, :]
    spare = jnp.concatenate(
        [total_wide[:, i * WIDTH : (i + 1) * WIDTH] for i in range(INNER // WIDTH)], axis=0
    )
    parts = pieces_ref.shape[0]
    per = N // parts
    for d in range(parts):
        pieces_ref[d, :, :INNER] = state[d * per : (d + 1) * per, :]
        pieces_ref[d, 0:4, INNER:] = spare
        if per > 4:
            pieces_ref[d, 4:, INNER:] = jnp.zeros((per - 4, WIDTH), F32)


def local_kernel(
    xbc_ref, normed_ref, inverse_ref, step_ref, run_ref, w_in_ref, pad_proj_ref, a_log_ref, skip_ref,
    out_ref, silu_ref, w_ref, sems,
):
    copies = [
        pltpu.make_async_copy(w_in_ref.at[:, 256 * t : 256 * (t + 1)], w_ref.at[t], sems.at[t])
        for t in range(INNER // 256)
    ]
    for copy in copies:
        copy.start()
    split = jnp.concatenate(thirds(log_decays(step_ref[...], a_log_ref)), axis=1)
    upper = (iota((CAP, CAP), 0) <= iota((CAP, CAP), 1)).astype(BF16)
    run_t = sum_thirds(dot(split, upper, ((0,), (0,))), 0)
    state = jnp.zeros((N, INNER), F32)
    skip = spread_heads(jnp.broadcast_to(line(skip_ref), (8, HEADS_HERE)))[0:1, :]
    start_run = jnp.zeros((1, HEADS_HERE), F32)
    for start, length in CHUNKS:
        rows = slice(start, start + length)
        x = xbc_ref[rows, :INNER]
        b = xbc_ref[rows, INNER : INNER + N]
        c = xbc_ref[rows, INNER + N :]
        run = run_ref[rows, :]
        step = step_ref[rows, :]
        end_run = run[length - 1 :, :]
        scaled = (x * spread_heads(step)).astype(BF16)
        inter = dot3(c, b, ((1,), (1,)))
        lower = iota((length, length), 0) >= iota((length, length), 1)
        outs = []
        for k in range(HEADS_HERE):
            gap = run[:, k : k + 1] - run_t[k : k + 1, rows]
            w = inter * jnp.exp(jnp.where(lower, gap, LOW))
            outs.append(dot(w.astype(BF16), scaled[:, k * P_SIZE : (k + 1) * P_SIZE]))
        y = jnp.concatenate(outs, axis=1) + skip * x
        if start > 0:
            y = y + spread_heads(jnp.exp(run - start_run)) * dot3(c, state)
        out_ref[rows, :] = y
        if start + length < CAP:
            weighted = x * spread_heads(step * jnp.exp(end_run - run))
            kept = spread_heads(jnp.broadcast_to(jnp.exp(end_run - start_run), (8, HEADS_HERE)))
            state = state * kept[0:1, :] + dot3(b, weighted, ((0,), (0,)))
        start_run = end_run
    pad_proj = line(pad_proj_ref)
    for t in range(INNER // 256):
        copies[t].wait()
        lanes = slice(256 * t, 256 * (t + 1))
        gate = dot(normed_ref[...], w_ref[t]) + inverse_ref[...] * pad_proj[:, lanes]
        silu_ref[:, lanes] = gate / (1.0 + jnp.exp(-gate))


def scan_kernel(got_ref, before_ref):
    act, per, _ = got_ref.shape
    state = jnp.zeros((per, INNER), F32)
    for j in range(act):
        before_ref[j] = state
        keep = jnp.exp(got_ref[j, 0:4, INNER:])
        keep = jnp.concatenate([keep[i : i + 1, :] for i in range(INNER // WIDTH)], axis=1)
        state = state * keep + got_ref[j, :, :INNER]


def output_kernel(
    run_ref, state_ref, gain_ref, xbc_ref, local_ref, silu_ref, w_out_ref,
    out_ref, full_ref, c_ref, local_v, silu_v, w_ref, sems,
):
    copies = [
        pltpu.make_async_copy(given, held, sems.at[i])
        for i, (given, held) in enumerate(
            (
                (xbc_ref.at[:, INNER + N :], c_ref),
                (local_ref, local_v),
                (silu_ref, silu_v),
                (w_out_ref, w_ref),
            )
        )
    ]
    for copy in copies:
        copy.start()
    parts, per, _ = state_ref.shape
    for d in range(parts):
        full_ref[d * per : (d + 1) * per, :] = state_ref[d]
    decay = spread_heads(jnp.exp(run_ref[...]))
    copies[0].wait()
    carried = decay * dot3(c_ref[...], full_ref[...])
    copies[1].wait()
    copies[2].wait()
    gated = (local_v[...] + carried) * silu_v[...]
    power = jnp.mean(gated * gated, axis=1, keepdims=True)
    mixed = (gated * lax.rsqrt(power + eps) * line(gain_ref)).astype(BF16)
    copies[3].wait()
    for i in range(HEAD_PARTS // 2):
        pair = dot(mixed, w_ref[:, i * 2 * WIDTH : (i + 1) * 2 * WIDTH]).astype(BF16)
        out_ref[2 * i] = pair[:, :WIDTH]
        out_ref[2 * i + 1] = pair[:, WIDTH:]


def main_kernel(packed_ref, parts_ref, carry_ref, kept_ref, main_ref, sent_ref):
    summed = packed_ref[...].astype(F32)
    added = parts_ref[0].astype(F32)
    for i in range(1, HEAD_PARTS):
        added = added + parts_ref[i].astype(F32)
    main = (summed + added).astype(BF16)
    main_ref[...] = main
    split = jnp.concatenate([jnp.broadcast_to(p, (8, CAP)) for p in thirds(carry_ref[...])], axis=0)
    sums = dot(split, main)
    carry = sums[0:1] + sums[8:9] + sums[16:17]
    row = jnp.concatenate([carry, kept_ref[...]], axis=0)
    sent_ref[...] = jnp.broadcast_to(row[None], sent_ref.shape)


def decode_kernel(enc_ref, w_hi_ref, w_lo_ref, main_ref, decay_ref, carries_ref, out_ref):
    me = lax.axis_index("act")
    act = carries_ref.shape[0]
    carry = jnp.zeros((1, WIDTH), F32)
    for j in range(act):
        after = carry * jnp.exp(carries_ref[j, 1:2, :]) + carries_ref[j, 0:1, :]
        carry = jnp.where(j < me, after, carry)
    main = main_ref[...]
    smoothed = dot(w_hi_ref[...], main) + dot(w_lo_ref[...], main) + decay_ref[...] * carry
    out_ref[...] = (enc_ref[...].astype(F32) + smoothed).astype(BF16)


def shape(dims, dtype=F32):
    return jax.ShapeDtypeStruct(dims, dtype)


def call(kernel, outs, name, specs=None, scratch=(), flops=0, transcendentals=0, nbytes=0):
    more = {} if specs is None else {"in_specs": specs}
    return pl.pallas_call(
        kernel,
        out_shape=outs,
        name=name,
        scratch_shapes=scratch,
        compiler_params=pltpu.CompilerParams(vmem_limit_bytes=VMEM_LIMIT),
        cost_estimate=pl.CostEstimate(
            flops=flops, transcendentals=transcendentals, bytes_accessed=nbytes
        ),
        **more,
    )


def body(
    enc_rows,
    boundary_flags,
    boundary_prob,
    pad_vector,
    norm_gain,
    w_in,
    w_dt,
    pad_proj,
    pad_dt,
    dt_bias,
    a_log,
    d_skip,
    gate_gain,
    w_out,
):
    act = lax.axis_size("act")
    held, apart = pl.BlockSpec(), pl.BlockSpec(memory_space=pltpu.HBM)
    packed = call(select_kernel, shape((CAP, WIDTH), BF16), "select", flops=10**8)(boundary_flags, enc_rows)
    rows = lax.all_gather(packed, "head", axis=1, tiled=True)

    w_hi, w_lo, carry_w, kept, decay = call(
        weights_kernel,
        (
            shape((BYTES, CAP), BF16),
            shape((BYTES, CAP), BF16),
            shape((1, CAP)),
            shape((1, WIDTH)),
            shape((BYTES, 1)),
        ),
        "weights",
        transcendentals=BYTES * CAP,
        flops=BYTES * CAP * 30,
        nbytes=10**6,
    )(boundary_flags, boundary_prob)

    xbc, normed, inverse, step, run, pieces = call(
        project_kernel,
        (
            shape((CAP, XBC)),
            shape((CAP, D), BF16),
            shape((CAP, 1)),
            shape((CAP, HEADS_HERE)),
            shape((CAP, HEADS_HERE)),
            shape((act, N // act, INNER + WIDTH)),
        ),
        "project",
        specs=[held] * 4 + [apart] + [held] * 5,
        scratch=[pltpu.VMEM((XBC // 256, D, 256), BF16), pltpu.SemaphoreType.DMA((XBC // 256,))],
        flops=2 * CAP * D * XBC,
        nbytes=8 * 10**6,
    )(rows, boundary_flags, pad_vector, norm_gain, w_in, w_dt.T, pad_proj, pad_dt, dt_bias, a_log)

    got = lax.all_to_all(pieces, "act", 0, 0)
    local, silu = call(
        local_kernel,
        (shape((CAP, INNER)), shape((CAP, INNER))),
        "local",
        specs=[held] * 5 + [apart] + [held] * 3,
        scratch=[pltpu.VMEM((INNER // 256, D, 256), BF16), pltpu.SemaphoreType.DMA((INNER // 256,))],
        flops=2 * 10**9,
        transcendentals=CAP * 2048,
        nbytes=6 * 10**6,
    )(xbc, normed, inverse, step, run, w_in, pad_proj, a_log, d_skip)
    before = call(scan_kernel, shape((act, N // act, INNER)), "scan", nbytes=6 * 10**5)(got)
    state_in = lax.all_to_all(before, "act", 0, 0)

    partial = call(
        output_kernel,
        shape((HEAD_PARTS, CAP, WIDTH), BF16),
        "output",
        specs=[held] * 3 + [apart] * 4,
        scratch=[
            pltpu.VMEM((N, INNER), F32),
            pltpu.VMEM((CAP, N), F32),
            pltpu.VMEM((CAP, INNER), F32),
            pltpu.VMEM((CAP, INNER), F32),
            pltpu.VMEM((INNER, D), BF16),
            pltpu.SemaphoreType.DMA((4,)),
        ],
        flops=2 * CAP * INNER * D,
        nbytes=6 * 10**6,
    )(run, state_in, gate_gain, xbc, local, silu, w_out)

    parts = lax.all_to_all(partial, "head", 0, 0)
    main, carry = call(
        main_kernel, (shape((CAP, WIDTH), BF16), shape((act, 2, WIDTH))), "main", nbytes=6 * 10**5
    )(packed, parts, carry_w, kept)
    carries = lax.all_to_all(carry, "act", 0, 0)
    return call(
        decode_kernel, shape((BYTES, WIDTH), BF16), "decode", flops=2 * 10**8, nbytes=2 * 10**6
    )(enc_rows, w_hi, w_lo, main, decay, carries)


def solution(mesh):
    seq, heads = mesh.shape["seq"], mesh.shape["head"]
    split = Mesh(mesh.devices.reshape(2, seq // 2, heads), ("half", "act", "head"))
    by_seq, by_head = ("half", "act"), "head"
    in_specs = (
        P(by_seq, by_head),
        P(by_seq),
        P(by_seq),
        P(),
        P(),
        P(None, by_head),
        P(None, by_head),
        P(by_head),
        P(by_head),
        P(by_head),
        P(by_head),
        P(by_head),
        P(by_head),
        P(by_head, None),
    )
    return jax.shard_map(
        body, mesh=split, in_specs=in_specs, out_specs=P(by_seq, by_head), check_vma=False
    )
```

```python
import jax
import jax.numpy as jnp
from jax import lax
from jax.experimental import pallas as pl
from jax.experimental.pallas import tpu as pltpu
from jax.sharding import Mesh
from jax.sharding import PartitionSpec as P

D = 1024
E = 2048
N = 128
HEADS_HERE = 8
P_SIZE = 64
INNER = HEADS_HERE * P_SIZE
COLS = 2 * INNER + 2 * N
CAP = 432
HEAD_PARTS = 8
BYTES = 576
WIDTH = 128
CHUNKS = ((0, 128), (128, 128), (256, 128), (384, 48))
LOW = -1e30
XBC = INNER + 2 * N
VMEM_LIMIT = 24 * 2**20
eps = 1e-05
F32 = jnp.float32
BF16 = jnp.bfloat16


def dot(a, b, contract=((1,), (0,))):
    return lax.dot_general(a, b, (contract, ((), ())), preferred_element_type=F32)


def halves(a):
    hi = a.astype(BF16)
    return hi, (a - hi.astype(F32)).astype(BF16)


def thirds(a):
    hi = a.astype(BF16)
    rest = a - hi.astype(F32)
    mid = rest.astype(BF16)
    return hi, mid, (rest - mid.astype(F32)).astype(BF16)


def dot3(a, b, contract=((1,), (0,))):
    a_hi, a_lo = halves(a)
    b_hi, b_lo = halves(b)
    return dot(a_hi, b_hi, contract) + dot(a_hi, b_lo, contract) + dot(a_lo, b_hi, contract)


def iota(shape, dim):
    return lax.broadcasted_iota(jnp.int32, shape, dim)


def spread_heads(a):
    owner = (iota((2 * HEADS_HERE, INNER), 1) // P_SIZE) == (
        iota((2 * HEADS_HERE, INNER), 0) % HEADS_HERE
    )
    hi, lo = halves(a)
    return dot(jnp.concatenate([hi, lo], axis=1), owner.astype(BF16))


def line(ref):
    return ref[...].reshape(1, ref.shape[0])


def fetch(given, held, sems):
    copies = [pltpu.make_async_copy(a, b, sems.at[i]) for i, (a, b) in enumerate(zip(given, held))]
    for copy in copies:
        copy.start()
    return copies


def arrived(copies):
    for copy in copies:
        copy.wait()


def select_kernel(flags_hbm, enc_hbm, packed_ref, flags_ref, enc_ref, sems):
    copies = fetch((flags_hbm, enc_hbm), (flags_ref, enc_ref), sems)
    arrived(copies)
    flags = line(flags_ref)
    upper = (iota((BYTES, BYTES), 0) <= iota((BYTES, BYTES), 1)).astype(BF16)
    rank = dot(flags.astype(F32).astype(BF16), upper)
    place = jnp.where(flags > 0, rank.astype(jnp.int32) - 1, -1)
    hit = (iota((CAP, BYTES), 0) == place).astype(F32).astype(BF16)
    packed_ref[...] = dot(hit, enc_ref[...]).astype(BF16)


def weights_kernel(flags_ref, prob_ref, w_hi_ref, w_lo_ref, carry_ref, kept_ref, decay_ref):
    flags = line(flags_ref).astype(F32)
    prob = prob_ref[...].astype(F32).reshape(1, BYTES)
    logs = jnp.where(flags > 0, jnp.log1p(-prob), 0.0)
    before = iota((BYTES, BYTES), 1) <= iota((BYTES, BYTES), 0)
    same = iota((BYTES, BYTES), 1) == iota((BYTES, BYTES), 0)

    def column(mask, row):
        return jnp.sum(jnp.where(mask, row, 0.0), axis=1, keepdims=True)

    rank = column(before, flags)
    kept = column(before, logs)
    flag = column(same, flags)
    chance = column(same, prob)
    place = iota((BYTES, CAP), 1).astype(F32)
    hit = (place == rank - 1.0) & (flag > 0)
    kept_k = jnp.sum(jnp.where(hit, kept, 0.0), axis=0, keepdims=True)
    prob_k = jnp.sum(jnp.where(hit, chance, 0.0), axis=0, keepdims=True)
    gap = jnp.where(place < rank, kept - kept_k, LOW)
    hi, lo = halves(jnp.exp(gap) * prob_k)
    w_hi_ref[...] = hi
    w_lo_ref[...] = lo
    total = jnp.sum(logs, axis=1, keepdims=True)
    count = jnp.sum(flags, axis=1, keepdims=True)
    real = iota((1, CAP), 1).astype(F32) < count
    carry_ref[...] = jnp.exp(jnp.where(real, total - kept_k, LOW)) * prob_k
    kept_ref[...] = jnp.broadcast_to(total, (1, WIDTH))
    decay_ref[...] = jnp.exp(kept)


def log_decays(step, a_log_ref):
    return -jnp.exp(line(a_log_ref)) * step


def sum_thirds(sums, axis):
    h = HEADS_HERE
    if axis == 0:
        return sums[:h] + sums[h : 2 * h] + sums[2 * h :]
    return sums[:, :h] + sums[:, h : 2 * h] + sums[:, 2 * h :]


def project_kernel(
    rows_ref, w_in_ref, *refs,
):
    given, refs = refs[:8], refs[8:]
    (xbc_ref, normed_ref, inverse_ref, step_ref, run_ref, pieces_ref), refs = refs[:6], refs[6:]
    held, (w_ref, sems, small_sems) = refs[:8], refs[8:]
    flags_ref, pad_ref, gain_ref, w_dt_ref, pad_proj_ref, pad_dt_ref, bias_ref, a_log_ref = held
    small = fetch(given, held, small_sems)
    tiles = range(XBC // 256)
    copies = [
        pltpu.make_async_copy(
            w_in_ref.at[:, INNER + 256 * t : INNER + 256 * (t + 1)], w_ref.at[t], sems.at[t]
        )
        for t in tiles
    ]
    for copy in copies:
        copy.start()
    energy = jnp.zeros((CAP, WIDTH), F32)
    for i in range(HEAD_PARTS):
        wide = rows_ref[:, i * WIDTH : (i + 1) * WIDTH].astype(F32)
        energy = energy + wide * wide
    arrived(small)
    pad = line(pad_ref)
    power = jnp.sum(energy, axis=1, keepdims=True) + jnp.sum(pad * pad)
    inverse = lax.rsqrt(power / E + eps)
    inverse_ref[...] = inverse
    gain = line(gain_ref)
    for i in range(HEAD_PARTS):
        lanes = slice(i * WIDTH, (i + 1) * WIDTH)
        normed_ref[:, lanes] = (rows_ref[:, lanes].astype(F32) * inverse * gain[:, lanes]).astype(BF16)
    h = HEADS_HERE
    raw = dot(normed_ref[...], w_dt_ref[...], ((1,), (1,))) + inverse * line(pad_dt_ref) + line(bias_ref)
    soft = jnp.maximum(raw, 0.0) + jnp.log1p(jnp.exp(-jnp.abs(raw)))
    count = jnp.sum(line(flags_ref).astype(F32), axis=1, keepdims=True)
    step = jnp.where(iota((CAP, h), 0).astype(F32) < count, soft, 0.0)
    step_ref[...] = step
    split = jnp.concatenate(thirds(log_decays(step, a_log_ref)), axis=1)
    lower = (iota((CAP, CAP), 1) <= iota((CAP, CAP), 0)).astype(BF16)
    run = sum_thirds(dot(lower, split), 1)
    run_ref[...] = run
    total = run[CAP - 1 :, :]
    tail = spread_heads(jnp.exp(total - run) * step)
    pad_proj = line(pad_proj_ref)
    for t in tiles:
        copies[t].wait()
        lanes = slice(256 * t, 256 * (t + 1))
        offset = inverse * pad_proj[:, INNER + 256 * t : INNER + 256 * (t + 1)]
        xbc_ref[:, lanes] = dot(normed_ref[...], w_ref[t]) + offset
    state = dot3(xbc_ref[:, INNER : INNER + N], xbc_ref[:, :INNER] * tail, ((0,), (0,)))
    total_wide = spread_heads(jnp.broadcast_to(total, (8, h)))[0:1, :]
    spare = jnp.concatenate(
        [total_wide[:, i * WIDTH : (i + 1) * WIDTH] for i in range(INNER // WIDTH)], axis=0
    )
    parts = pieces_ref.shape[0]
    per = N // parts
    for d in range(parts):
        pieces_ref[d, :, :INNER] = state[d * per : (d + 1) * per, :]
        pieces_ref[d, 0:4, INNER:] = spare
        if per > 4:
            pieces_ref[d, 4:, INNER:] = jnp.zeros((per - 4, WIDTH), F32)


def local_kernel(*refs):
    given, w_in_ref, (out_ref, silu_ref), held, (w_ref, sems) = refs[:8], refs[8], refs[9:11], refs[11:19], refs[19:]
    xbc_ref, normed_ref, inverse_ref, step_ref, run_ref, pad_proj_ref, a_log_ref, skip_ref = held
    tiles = range(INNER // 256)
    pieces = [w_in_ref.at[:, 256 * t : 256 * (t + 1)] for t in tiles]
    copies = fetch(given + tuple(pieces), held + tuple(w_ref.at[t] for t in tiles), sems)
    arrived(copies[:8])
    copies = copies[8:]
    split = jnp.concatenate(thirds(log_decays(step_ref[...], a_log_ref)), axis=1)
    upper = (iota((CAP, CAP), 0) <= iota((CAP, CAP), 1)).astype(BF16)
    run_t = sum_thirds(dot(split, upper, ((0,), (0,))), 0)
    state = jnp.zeros((N, INNER), F32)
    skip = spread_heads(jnp.broadcast_to(line(skip_ref), (8, HEADS_HERE)))[0:1, :]
    start_run = jnp.zeros((1, HEADS_HERE), F32)
    for start, length in CHUNKS:
        rows = slice(start, start + length)
        x = xbc_ref[rows, :INNER]
        b = xbc_ref[rows, INNER : INNER + N]
        c = xbc_ref[rows, INNER + N :]
        run = run_ref[rows, :]
        step = step_ref[rows, :]
        end_run = run[length - 1 :, :]
        scaled = (x * spread_heads(step)).astype(BF16)
        inter = dot3(c, b, ((1,), (1,)))
        lower = iota((length, length), 0) >= iota((length, length), 1)
        outs = []
        for k in range(HEADS_HERE):
            gap = run[:, k : k + 1] - run_t[k : k + 1, rows]
            w = inter * jnp.exp(jnp.where(lower, gap, LOW))
            outs.append(dot(w.astype(BF16), scaled[:, k * P_SIZE : (k + 1) * P_SIZE]))
        y = jnp.concatenate(outs, axis=1) + skip * x
        if start > 0:
            y = y + spread_heads(jnp.exp(run - start_run)) * dot3(c, state)
        out_ref[rows, :] = y.astype(BF16)
        if start + length < CAP:
            weighted = x * spread_heads(step * jnp.exp(end_run - run))
            kept = spread_heads(jnp.broadcast_to(jnp.exp(end_run - start_run), (8, HEADS_HERE)))
            state = state * kept[0:1, :] + dot3(b, weighted, ((0,), (0,)))
        start_run = end_run
    pad_proj = line(pad_proj_ref)
    for t in range(INNER // 256):
        copies[t].wait()
        lanes = slice(256 * t, 256 * (t + 1))
        gate = dot(normed_ref[...], w_ref[t]) + inverse_ref[...] * pad_proj[:, lanes]
        silu_ref[:, lanes] = (gate / (1.0 + jnp.exp(-gate))).astype(BF16)


def scan_kernel(got_ref, before_ref):
    act, per, _ = got_ref.shape
    state = jnp.zeros((per, INNER), F32)
    for j in range(act):
        before_ref[j] = state
        keep = jnp.exp(got_ref[j, 0:4, INNER:])
        keep = jnp.concatenate([keep[i : i + 1, :] for i in range(INNER // WIDTH)], axis=1)
        state = state * keep + got_ref[j, :, :INNER]


def output_kernel(
    state_ref, c_hbm, run_hbm, local_hbm, silu_hbm, gain_hbm, w_out_hbm,
    out_ref, full_ref, c_ref, run_ref, local_ref, silu_ref, gain_ref, w_ref, sems,
):
    copies = fetch(
        (c_hbm.at[:, INNER + N :], run_hbm, local_hbm, silu_hbm, gain_hbm, w_out_hbm),
        (c_ref, run_ref, local_ref, silu_ref, gain_ref, w_ref),
        sems,
    )
    parts, per, _ = state_ref.shape
    for d in range(parts):
        full_ref[d * per : (d + 1) * per, :] = state_ref[d]
    arrived(copies[:2])
    carried = spread_heads(jnp.exp(run_ref[...])) * dot3(c_ref[...], full_ref[...])
    arrived(copies[2:5])
    gated = (local_ref[...].astype(F32) + carried) * silu_ref[...].astype(F32)
    power = jnp.mean(gated * gated, axis=1, keepdims=True)
    mixed = (gated * lax.rsqrt(power + eps) * line(gain_ref)).astype(BF16)
    arrived(copies[5:])
    for i in range(HEAD_PARTS // 2):
        pair = dot(mixed, w_ref[:, i * 2 * WIDTH : (i + 1) * 2 * WIDTH]).astype(BF16)
        out_ref[2 * i] = pair[:, :WIDTH]
        out_ref[2 * i + 1] = pair[:, WIDTH:]


def main_kernel(packed_ref, parts_ref, carry_ref, kept_ref, main_ref, sent_ref):
    summed = packed_ref[...].astype(F32)
    added = parts_ref[0].astype(F32)
    for i in range(1, HEAD_PARTS):
        added = added + parts_ref[i].astype(F32)
    main = (summed + added).astype(BF16)
    main_ref[...] = main
    split = jnp.concatenate([jnp.broadcast_to(p, (8, CAP)) for p in thirds(carry_ref[...])], axis=0)
    sums = dot(split, main)
    carry = sums[0:1] + sums[8:9] + sums[16:17]
    row = jnp.concatenate([carry, kept_ref[...]], axis=0)
    sent_ref[...] = jnp.broadcast_to(row[None], sent_ref.shape)


def decode_kernel(enc_hbm, w_hi_ref, w_lo_ref, main_ref, decay_ref, carries_ref, out_ref, enc_ref, sems):
    copies = fetch((enc_hbm,), (enc_ref,), sems)
    me = lax.axis_index("act")
    act = carries_ref.shape[0]
    carry = jnp.zeros((1, WIDTH), F32)
    for j in range(act):
        after = carry * jnp.exp(carries_ref[j, 1:2, :]) + carries_ref[j, 0:1, :]
        carry = jnp.where(j < me, after, carry)
    main = main_ref[...]
    smoothed = dot(w_hi_ref[...], main) + dot(w_lo_ref[...], main) + decay_ref[...] * carry
    arrived(copies)
    out_ref[...] = (enc_ref[...].astype(F32) + smoothed).astype(BF16)


def shape(dims, dtype=F32):
    return jax.ShapeDtypeStruct(dims, dtype)


def call(kernel, outs, name, specs=None, scratch=(), flops=0, transcendentals=0, nbytes=0):
    more = {} if specs is None else {"in_specs": specs}
    run = pl.pallas_call(
        kernel,
        out_shape=outs,
        name=name,
        scratch_shapes=scratch,
        compiler_params=pltpu.CompilerParams(vmem_limit_bytes=VMEM_LIMIT),
        cost_estimate=pl.CostEstimate(
            flops=flops, transcendentals=transcendentals, bytes_accessed=nbytes
        ),
        **more,
    )
    if specs is None:
        return run
    return lambda *args: run(
        *[
            pltpu.with_memory_space_constraint(a, pltpu.HBM) if spec.memory_space == pltpu.HBM else a
            for a, spec in zip(args, specs)
        ]
    )


def body(
    enc_rows,
    boundary_flags,
    boundary_prob,
    pad_vector,
    norm_gain,
    w_in,
    w_dt,
    pad_proj,
    pad_dt,
    dt_bias,
    a_log,
    d_skip,
    gate_gain,
    w_out,
):
    act = lax.axis_size("act")
    held, apart = pl.BlockSpec(), pl.BlockSpec(memory_space=pltpu.HBM)
    dma = pltpu.SemaphoreType.DMA
    packed = call(
        select_kernel,
        shape((CAP, WIDTH), BF16),
        "select",
        specs=[apart] * 2,
        scratch=[pltpu.VMEM((BYTES,), jnp.int32), pltpu.VMEM((BYTES, WIDTH), BF16), dma((2,))],
        flops=10**8,
    )(boundary_flags, enc_rows)
    rows = lax.all_gather(packed, "head", axis=1, tiled=True)

    w_hi, w_lo, carry_w, kept, decay = call(
        weights_kernel,
        (
            shape((BYTES, CAP), BF16),
            shape((BYTES, CAP), BF16),
            shape((1, CAP)),
            shape((1, WIDTH)),
            shape((BYTES, 1)),
        ),
        "weights",
        transcendentals=BYTES * CAP,
        flops=BYTES * CAP * 30,
        nbytes=10**6,
    )(boundary_flags, boundary_prob)

    small = [boundary_flags, pad_vector, norm_gain, w_dt.T, pad_proj, pad_dt, dt_bias, a_log]
    xbc, normed, inverse, step, run, pieces = call(
        project_kernel,
        (
            shape((CAP, XBC)),
            shape((CAP, D), BF16),
            shape((CAP, 1)),
            shape((CAP, HEADS_HERE)),
            shape((CAP, HEADS_HERE)),
            shape((act, N // act, INNER + WIDTH)),
        ),
        "project",
        specs=[held] + [apart] * (1 + len(small)),
        scratch=[pltpu.VMEM(a.shape, a.dtype) for a in small]
        + [pltpu.VMEM((XBC // 256, D, 256), BF16), dma((XBC // 256,)), dma((len(small),))],
        flops=2 * CAP * D * XBC,
        nbytes=8 * 10**6,
    )(rows, w_in, *small)

    got = lax.all_to_all(pieces, "act", 0, 0)
    needed = [xbc, normed, inverse, step, run, pad_proj, a_log, d_skip]
    local, silu = call(
        local_kernel,
        (shape((CAP, INNER), BF16), shape((CAP, INNER), BF16)),
        "local",
        specs=[apart] * (len(needed) + 1),
        scratch=[pltpu.VMEM(a.shape, a.dtype) for a in needed]
        + [pltpu.VMEM((INNER // 256, D, 256), BF16), dma((len(needed) + INNER // 256,))],
        flops=2 * 10**9,
        transcendentals=CAP * 2048,
        nbytes=6 * 10**6,
    )(*needed, w_in)
    before = call(scan_kernel, shape((act, N // act, INNER)), "scan", nbytes=6 * 10**5)(got)
    state_in = lax.all_to_all(before, "act", 0, 0)

    partial = call(
        output_kernel,
        shape((HEAD_PARTS, CAP, WIDTH), BF16),
        "output",
        specs=[held] + [apart] * 6,
        scratch=[
            pltpu.VMEM((N, INNER), F32),
            pltpu.VMEM((CAP, N), F32),
            pltpu.VMEM((CAP, HEADS_HERE), F32),
            pltpu.VMEM((CAP, INNER), BF16),
            pltpu.VMEM((CAP, INNER), BF16),
            pltpu.VMEM((INNER,), F32),
            pltpu.VMEM((INNER, D), BF16),
            dma((6,)),
        ],
        flops=2 * CAP * INNER * D,
        nbytes=6 * 10**6,
    )(state_in, xbc, run, local, silu, gate_gain, w_out)

    parts = lax.all_to_all(partial, "head", 0, 0)
    main, carry = call(
        main_kernel, (shape((CAP, WIDTH), BF16), shape((act, 2, WIDTH))), "main", nbytes=6 * 10**5
    )(packed, parts, carry_w, kept)
    carries = lax.all_to_all(carry, "act", 0, 0)
    return call(
        decode_kernel,
        shape((BYTES, WIDTH), BF16),
        "decode",
        specs=[apart] + [held] * 5,
        scratch=[pltpu.VMEM((BYTES, WIDTH), BF16), dma((1,))],
        flops=2 * 10**8,
        nbytes=2 * 10**6,
    )(enc_rows, w_hi, w_lo, main, decay, carries)


def solution(mesh):
    seq, heads = mesh.shape["seq"], mesh.shape["head"]
    split = Mesh(mesh.devices.reshape(2, seq // 2, heads), ("half", "act", "head"))
    by_seq, by_head = ("half", "act"), "head"
    in_specs = (
        P(by_seq, by_head),
        P(by_seq),
        P(by_seq),
        P(),
        P(),
        P(None, by_head),
        P(None, by_head),
        P(by_head),
        P(by_head),
        P(by_head),
        P(by_head),
        P(by_head),
        P(by_head),
        P(by_head, None),
    )
    return jax.shard_map(
        body, mesh=split, in_specs=in_specs, out_specs=P(by_seq, by_head), check_vma=False
    )
```

```python
import jax
import jax.numpy as jnp
from jax import lax
from jax.experimental import pallas as pl
from jax.experimental.pallas import tpu as pltpu
from jax.sharding import Mesh
from jax.sharding import PartitionSpec as P

D = 1024
E = 2048
N = 128
HEADS_HERE = 8
P_SIZE = 64
INNER = HEADS_HERE * P_SIZE
COLS = 2 * INNER + 2 * N
CAP = 432
HEAD_PARTS = 8
BYTES = 576
WIDTH = 128
CHUNKS = ((0, 128), (128, 128), (256, 128), (384, 48))
LOW = -1e30
XBC = INNER + 2 * N
VMEM_LIMIT = 24 * 2**20
eps = 1e-05
F32 = jnp.float32
BF16 = jnp.bfloat16


def dot(a, b, contract=((1,), (0,))):
    return lax.dot_general(a, b, (contract, ((), ())), preferred_element_type=F32)


def halves(a):
    hi = a.astype(BF16)
    return hi, (a - hi.astype(F32)).astype(BF16)


def thirds(a):
    hi = a.astype(BF16)
    rest = a - hi.astype(F32)
    mid = rest.astype(BF16)
    return hi, mid, (rest - mid.astype(F32)).astype(BF16)


def dot3(a, b, contract=((1,), (0,))):
    a_hi, a_lo = halves(a)
    b_hi, b_lo = halves(b)
    return dot(a_hi, b_hi, contract) + dot(a_hi, b_lo, contract) + dot(a_lo, b_hi, contract)


def iota(shape, dim):
    return lax.broadcasted_iota(jnp.int32, shape, dim)


def spread_heads(a):
    owner = (iota((2 * HEADS_HERE, INNER), 1) // P_SIZE) == (
        iota((2 * HEADS_HERE, INNER), 0) % HEADS_HERE
    )
    hi, lo = halves(a)
    return dot(jnp.concatenate([hi, lo], axis=1), owner.astype(BF16))


def line(ref):
    return ref[...].reshape(1, ref.shape[0])


def fetch(given, held, sems, first=0):
    copies = [
        pltpu.make_async_copy(a, b, sems.at[first + i]) for i, (a, b) in enumerate(zip(given, held))
    ]
    for copy in copies:
        copy.start()
    return copies


def arrived(copies):
    for copy in copies:
        copy.wait()


def select_kernel(flags_hbm, enc_hbm, packed_ref, flags_ref, enc_ref, sems):
    copies = fetch((flags_hbm, enc_hbm), (flags_ref, enc_ref), sems)
    arrived(copies)
    flags = line(flags_ref)
    upper = (iota((BYTES, BYTES), 0) <= iota((BYTES, BYTES), 1)).astype(BF16)
    rank = dot(flags.astype(F32).astype(BF16), upper)
    place = jnp.where(flags > 0, rank.astype(jnp.int32) - 1, -1)
    hit = (iota((CAP, BYTES), 0) == place).astype(F32).astype(BF16)
    packed_ref[...] = dot(hit, enc_ref[...]).astype(BF16)


def weights_kernel(flags_ref, prob_ref, w_hi_ref, w_lo_ref, carry_ref, kept_ref, decay_ref):
    flags = line(flags_ref).astype(F32)
    prob = prob_ref[...].astype(F32).reshape(1, BYTES)
    logs = jnp.where(flags > 0, jnp.log1p(-prob), 0.0)
    before = iota((BYTES, BYTES), 1) <= iota((BYTES, BYTES), 0)
    same = iota((BYTES, BYTES), 1) == iota((BYTES, BYTES), 0)

    def column(mask, row):
        return jnp.sum(jnp.where(mask, row, 0.0), axis=1, keepdims=True)

    rank = column(before, flags)
    kept = column(before, logs)
    flag = column(same, flags)
    chance = column(same, prob)
    place = iota((BYTES, CAP), 1).astype(F32)
    hit = (place == rank - 1.0) & (flag > 0)
    kept_k = jnp.sum(jnp.where(hit, kept, 0.0), axis=0, keepdims=True)
    prob_k = jnp.sum(jnp.where(hit, chance, 0.0), axis=0, keepdims=True)
    gap = jnp.where(place < rank, kept - kept_k, LOW)
    hi, lo = halves(jnp.exp(gap) * prob_k)
    w_hi_ref[...] = hi
    w_lo_ref[...] = lo
    total = jnp.sum(logs, axis=1, keepdims=True)
    count = jnp.sum(flags, axis=1, keepdims=True)
    real = iota((1, CAP), 1).astype(F32) < count
    carry_ref[...] = jnp.exp(jnp.where(real, total - kept_k, LOW)) * prob_k
    kept_ref[...] = jnp.broadcast_to(total, (1, WIDTH))
    decay_ref[...] = jnp.exp(kept)


def log_decays(step, a_log_ref):
    return -jnp.exp(line(a_log_ref)) * step


def sum_thirds(sums, axis):
    h = HEADS_HERE
    if axis == 0:
        return sums[:h] + sums[h : 2 * h] + sums[2 * h :]
    return sums[:, :h] + sums[:, h : 2 * h] + sums[:, 2 * h :]


def project_kernel(
    rows_ref, w_in_ref, *refs,
):
    given, refs = refs[:8], refs[8:]
    (xbc_hbm, normed_hbm, aux_hbm, pieces_ref), refs = refs[:4], refs[4:]
    held, (xbc_ref, normed_ref, aux_ref, w_ref, sems, small_sems, out_sems) = refs[:8], refs[8:]
    flags_ref, pad_ref, gain_ref, w_dt_ref, pad_proj_ref, pad_dt_ref, bias_ref, a_log_ref = held
    small = fetch(given, held, small_sems)
    tiles = range(XBC // 256)
    copies = [
        pltpu.make_async_copy(
            w_in_ref.at[:, INNER + 256 * t : INNER + 256 * (t + 1)], w_ref.at[t], sems.at[t]
        )
        for t in tiles
    ]
    for copy in copies:
        copy.start()
    energy = jnp.zeros((CAP, WIDTH), F32)
    for i in range(HEAD_PARTS):
        wide = rows_ref[:, i * WIDTH : (i + 1) * WIDTH].astype(F32)
        energy = energy + wide * wide
    arrived(small)
    pad = line(pad_ref)
    power = jnp.sum(energy, axis=1, keepdims=True) + jnp.sum(pad * pad)
    inverse = lax.rsqrt(power / E + eps)
    gain = line(gain_ref)
    for i in range(HEAD_PARTS):
        lanes = slice(i * WIDTH, (i + 1) * WIDTH)
        normed_ref[:, lanes] = (rows_ref[:, lanes].astype(F32) * inverse * gain[:, lanes]).astype(BF16)
    kept = [pltpu.make_async_copy(normed_ref, normed_hbm, out_sems.at[0])]
    kept[0].start()
    h = HEADS_HERE
    raw = dot(normed_ref[...], w_dt_ref[...], ((1,), (1,))) + inverse * line(pad_dt_ref) + line(bias_ref)
    soft = jnp.maximum(raw, 0.0) + jnp.log1p(jnp.exp(-jnp.abs(raw)))
    count = jnp.sum(line(flags_ref).astype(F32), axis=1, keepdims=True)
    step = jnp.where(iota((CAP, h), 0).astype(F32) < count, soft, 0.0)
    split = jnp.concatenate(thirds(log_decays(step, a_log_ref)), axis=1)
    lower = (iota((CAP, CAP), 1) <= iota((CAP, CAP), 0)).astype(BF16)
    run = sum_thirds(dot(lower, split), 1)
    fill = jnp.zeros((CAP, WIDTH - 2 * h - 1), F32)
    aux_ref[...] = jnp.concatenate([step, run, inverse, fill], axis=1)
    total = run[CAP - 1 :, :]
    tail = spread_heads(jnp.exp(total - run) * step)
    pad_proj = line(pad_proj_ref)
    for t in tiles:
        copies[t].wait()
        lanes = slice(256 * t, 256 * (t + 1))
        offset = inverse * pad_proj[:, INNER + 256 * t : INNER + 256 * (t + 1)]
        xbc_ref[:, lanes] = dot(normed_ref[...], w_ref[t]) + offset
    kept += fetch((xbc_ref, aux_ref), (xbc_hbm, aux_hbm), out_sems, 1)
    state = dot3(xbc_ref[:, INNER : INNER + N], xbc_ref[:, :INNER] * tail, ((0,), (0,)))
    total_wide = spread_heads(jnp.broadcast_to(total, (8, h)))[0:1, :]
    spare = jnp.concatenate(
        [total_wide[:, i * WIDTH : (i + 1) * WIDTH] for i in range(INNER // WIDTH)], axis=0
    )
    parts = pieces_ref.shape[0]
    per = N // parts
    for d in range(parts):
        pieces_ref[d, :, :INNER] = state[d * per : (d + 1) * per, :]
        pieces_ref[d, 0:4, INNER:] = spare
        if per > 4:
            pieces_ref[d, 4:, INNER:] = jnp.zeros((per - 4, WIDTH), F32)
    arrived(kept)


def local_kernel(*refs):
    given, w_in_ref, outs_hbm, held = refs[:6], refs[6], refs[7:9], refs[9:15]
    out_ref, silu_ref, w_ref, sems, out_sems = refs[15:]
    xbc_ref, normed_ref, aux_ref, pad_proj_ref, a_log_ref, skip_ref = held
    h = HEADS_HERE
    tiles = range(INNER // 256)
    pieces = [w_in_ref.at[:, 256 * t : 256 * (t + 1)] for t in tiles]
    copies = fetch(given + tuple(pieces), held + tuple(w_ref.at[t] for t in tiles), sems)
    arrived(copies[: len(held)])
    copies = copies[len(held) :]
    split = jnp.concatenate(thirds(log_decays(aux_ref[:, :h], a_log_ref)), axis=1)
    upper = (iota((CAP, CAP), 0) <= iota((CAP, CAP), 1)).astype(BF16)
    run_t = sum_thirds(dot(split, upper, ((0,), (0,))), 0)
    state = jnp.zeros((N, INNER), F32)
    skip = spread_heads(jnp.broadcast_to(line(skip_ref), (8, HEADS_HERE)))[0:1, :]
    start_run = jnp.zeros((1, HEADS_HERE), F32)
    for start, length in CHUNKS:
        rows = slice(start, start + length)
        x = xbc_ref[rows, :INNER]
        b = xbc_ref[rows, INNER : INNER + N]
        c = xbc_ref[rows, INNER + N :]
        step = aux_ref[rows, :h]
        run = aux_ref[rows, h : 2 * h]
        end_run = run[length - 1 :, :]
        scaled = (x * spread_heads(step)).astype(BF16)
        inter = dot3(c, b, ((1,), (1,)))
        lower = iota((length, length), 0) >= iota((length, length), 1)
        outs = []
        for k in range(HEADS_HERE):
            gap = run[:, k : k + 1] - run_t[k : k + 1, rows]
            w = inter * jnp.exp(jnp.where(lower, gap, LOW))
            outs.append(dot(w.astype(BF16), scaled[:, k * P_SIZE : (k + 1) * P_SIZE]))
        y = jnp.concatenate(outs, axis=1) + skip * x
        if start > 0:
            y = y + spread_heads(jnp.exp(run - start_run)) * dot3(c, state)
        out_ref[rows, :] = y.astype(BF16)
        if start + length < CAP:
            weighted = x * spread_heads(step * jnp.exp(end_run - run))
            kept = spread_heads(jnp.broadcast_to(jnp.exp(end_run - start_run), (8, HEADS_HERE)))
            state = state * kept[0:1, :] + dot3(b, weighted, ((0,), (0,)))
        start_run = end_run
    kept = fetch((out_ref,), outs_hbm[:1], out_sems)
    pad_proj = line(pad_proj_ref)
    inverse = aux_ref[:, 2 * h : 2 * h + 1]
    for t in range(INNER // 256):
        copies[t].wait()
        lanes = slice(256 * t, 256 * (t + 1))
        gate = dot(normed_ref[...], w_ref[t]) + inverse * pad_proj[:, lanes]
        silu_ref[:, lanes] = (gate / (1.0 + jnp.exp(-gate))).astype(BF16)
    kept += fetch((silu_ref,), outs_hbm[1:], out_sems, 1)
    arrived(kept)


def scan_kernel(got_ref, before_ref):
    act, per, _ = got_ref.shape
    state = jnp.zeros((per, INNER), F32)
    for j in range(act):
        before_ref[j] = state
        keep = jnp.exp(got_ref[j, 0:4, INNER:])
        keep = jnp.concatenate([keep[i : i + 1, :] for i in range(INNER // WIDTH)], axis=1)
        state = state * keep + got_ref[j, :, :INNER]


def output_kernel(
    state_ref, c_hbm, aux_hbm, local_hbm, silu_hbm, gain_hbm, w_out_hbm,
    out_ref, full_ref, c_ref, aux_ref, local_ref, silu_ref, gain_ref, w_ref, sems,
):
    copies = fetch(
        (c_hbm.at[:, INNER + N :], aux_hbm, local_hbm, silu_hbm, gain_hbm, w_out_hbm),
        (c_ref, aux_ref, local_ref, silu_ref, gain_ref, w_ref),
        sems,
    )
    parts, per, _ = state_ref.shape
    for d in range(parts):
        full_ref[d * per : (d + 1) * per, :] = state_ref[d]
    arrived(copies[:2])
    carried = spread_heads(jnp.exp(aux_ref[:, HEADS_HERE : 2 * HEADS_HERE])) * dot3(c_ref[...], full_ref[...])
    arrived(copies[2:5])
    gated = (local_ref[...].astype(F32) + carried) * silu_ref[...].astype(F32)
    power = jnp.mean(gated * gated, axis=1, keepdims=True)
    mixed = (gated * lax.rsqrt(power + eps) * line(gain_ref)).astype(BF16)
    arrived(copies[5:])
    for i in range(HEAD_PARTS // 2):
        pair = dot(mixed, w_ref[:, i * 2 * WIDTH : (i + 1) * 2 * WIDTH]).astype(BF16)
        out_ref[2 * i] = pair[:, :WIDTH]
        out_ref[2 * i + 1] = pair[:, WIDTH:]


def main_kernel(packed_ref, parts_ref, carry_ref, kept_ref, main_ref, sent_ref):
    summed = packed_ref[...].astype(F32)
    added = parts_ref[0].astype(F32)
    for i in range(1, HEAD_PARTS):
        added = added + parts_ref[i].astype(F32)
    main = (summed + added).astype(BF16)
    main_ref[...] = main
    split = jnp.concatenate([jnp.broadcast_to(p, (8, CAP)) for p in thirds(carry_ref[...])], axis=0)
    sums = dot(split, main)
    carry = sums[0:1] + sums[8:9] + sums[16:17]
    row = jnp.concatenate([carry, kept_ref[...]], axis=0)
    sent_ref[...] = jnp.broadcast_to(row[None], sent_ref.shape)


def decode_kernel(enc_ref, w_hi_ref, w_lo_ref, main_ref, decay_ref, carries_ref, out_ref):
    me = lax.axis_index("act")
    act = carries_ref.shape[0]
    carry = jnp.zeros((1, WIDTH), F32)
    for j in range(act):
        after = carry * jnp.exp(carries_ref[j, 1:2, :]) + carries_ref[j, 0:1, :]
        carry = jnp.where(j < me, after, carry)
    main = main_ref[...]
    smoothed = dot(w_hi_ref[...], main) + dot(w_lo_ref[...], main) + decay_ref[...] * carry
    out_ref[...] = (enc_ref[...].astype(F32) + smoothed).astype(BF16)


def shape(dims, dtype=F32):
    return jax.ShapeDtypeStruct(dims, dtype)


def call(kernel, outs, name, specs=None, out_specs=None, scratch=(), flops=0, transcendentals=0, nbytes=0):
    more = {} if specs is None else {"in_specs": specs}
    if out_specs is not None:
        more["out_specs"] = out_specs
    run = pl.pallas_call(
        kernel,
        out_shape=outs,
        name=name,
        scratch_shapes=scratch,
        compiler_params=pltpu.CompilerParams(vmem_limit_bytes=VMEM_LIMIT),
        cost_estimate=pl.CostEstimate(
            flops=flops, transcendentals=transcendentals, bytes_accessed=nbytes
        ),
        **more,
    )
    if specs is None:
        return run
    return lambda *args: run(
        *[
            pltpu.with_memory_space_constraint(a, pltpu.HBM) if spec.memory_space == pltpu.HBM else a
            for a, spec in zip(args, specs)
        ]
    )


def body(
    enc_rows,
    boundary_flags,
    boundary_prob,
    pad_vector,
    norm_gain,
    w_in,
    w_dt,
    pad_proj,
    pad_dt,
    dt_bias,
    a_log,
    d_skip,
    gate_gain,
    w_out,
):
    act = lax.axis_size("act")
    held, apart = pl.BlockSpec(), pl.BlockSpec(memory_space=pltpu.HBM)
    dma = pltpu.SemaphoreType.DMA
    packed = call(
        select_kernel,
        shape((CAP, WIDTH), BF16),
        "select",
        specs=[apart] * 2,
        scratch=[pltpu.VMEM((BYTES,), jnp.int32), pltpu.VMEM((BYTES, WIDTH), BF16), dma((2,))],
        flops=10**8,
    )(boundary_flags, enc_rows)
    rows = lax.all_gather(packed, "head", axis=1, tiled=True)

    w_hi, w_lo, carry_w, kept, decay = call(
        weights_kernel,
        (
            shape((BYTES, CAP), BF16),
            shape((BYTES, CAP), BF16),
            shape((1, CAP)),
            shape((1, WIDTH)),
            shape((BYTES, 1)),
        ),
        "weights",
        transcendentals=BYTES * CAP,
        flops=BYTES * CAP * 30,
        nbytes=10**6,
    )(boundary_flags, boundary_prob)

    small = [boundary_flags, pad_vector, norm_gain, w_dt.T, pad_proj, pad_dt, dt_bias, a_log]
    kept_across = [((CAP, XBC), F32), ((CAP, D), BF16), ((CAP, WIDTH), F32)]
    xbc, normed, aux, pieces = call(
        project_kernel,
        [pltpu.HBM(*a) for a in kept_across] + [shape((act, N // act, INNER + WIDTH))],
        "project",
        out_specs=[apart] * 3 + [held],
        specs=[held] + [apart] * (1 + len(small)),
        scratch=[pltpu.VMEM(a.shape, a.dtype) for a in small]
        + [pltpu.VMEM(*a) for a in kept_across]
        + [pltpu.VMEM((XBC // 256, D, 256), BF16), dma((XBC // 256,)), dma((len(small),)), dma((3,))],
        flops=2 * CAP * D * XBC,
        nbytes=8 * 10**6,
    )(rows, w_in, *small)

    got = lax.all_to_all(pieces, "act", 0, 0)
    needed = [xbc, normed, aux, pad_proj, a_log, d_skip]
    local, silu = call(
        local_kernel,
        [pltpu.HBM((CAP, INNER), BF16)] * 2,
        "local",
        out_specs=[apart] * 2,
        specs=[apart] * (len(needed) + 1),
        scratch=[pltpu.VMEM(a.shape, a.dtype) for a in needed]
        + [pltpu.VMEM((CAP, INNER), BF16)] * 2
        + [pltpu.VMEM((INNER // 256, D, 256), BF16), dma((len(needed) + INNER // 256,)), dma((2,))],
        flops=2 * 10**9,
        transcendentals=CAP * 2048,
        nbytes=6 * 10**6,
    )(*needed, w_in)
    before = call(scan_kernel, shape((act, N // act, INNER)), "scan", nbytes=6 * 10**5)(got)
    state_in = lax.all_to_all(before, "act", 0, 0)

    partial = call(
        output_kernel,
        shape((HEAD_PARTS, CAP, WIDTH), BF16),
        "output",
        specs=[held] + [apart] * 6,
        scratch=[
            pltpu.VMEM((N, INNER), F32),
            pltpu.VMEM((CAP, N), F32),
            pltpu.VMEM((CAP, WIDTH), F32),
            pltpu.VMEM((CAP, INNER), BF16),
            pltpu.VMEM((CAP, INNER), BF16),
            pltpu.VMEM((INNER,), F32),
            pltpu.VMEM((INNER, D), BF16),
            dma((6,)),
        ],
        flops=2 * CAP * INNER * D,
        nbytes=6 * 10**6,
    )(state_in, xbc, aux, local, silu, gate_gain, w_out)

    parts = lax.all_to_all(partial, "head", 0, 0)
    main, carry = call(
        main_kernel, (shape((CAP, WIDTH), BF16), shape((act, 2, WIDTH))), "main", nbytes=6 * 10**5
    )(packed, parts, carry_w, kept)
    carries = lax.all_to_all(carry, "act", 0, 0)
    return call(
        decode_kernel,
        shape((BYTES, WIDTH), BF16),
        "decode",
        flops=2 * 10**8,
        nbytes=2 * 10**6,
    )(enc_rows, w_hi, w_lo, main, decay, carries)


def solution(mesh):
    seq, heads = mesh.shape["seq"], mesh.shape["head"]
    split = Mesh(mesh.devices.reshape(2, seq // 2, heads), ("half", "act", "head"))
    by_seq, by_head = ("half", "act"), "head"
    in_specs = (
        P(by_seq, by_head),
        P(by_seq),
        P(by_seq),
        P(),
        P(),
        P(None, by_head),
        P(None, by_head),
        P(by_head),
        P(by_head),
        P(by_head),
        P(by_head),
        P(by_head),
        P(by_head),
        P(by_head, None),
    )
    return jax.shard_map(
        body, mesh=split, in_specs=in_specs, out_specs=P(by_seq, by_head), check_vma=False
    )
```

```python
import jax
import jax.numpy as jnp
from jax import lax
from jax.experimental import pallas as pl
from jax.experimental.pallas import tpu as pltpu
from jax.sharding import Mesh
from jax.sharding import PartitionSpec as P

D = 1024
E = 2048
N = 128
HEADS_HERE = 8
P_SIZE = 64
INNER = HEADS_HERE * P_SIZE
COLS = 2 * INNER + 2 * N
CAP = 432
HEAD_PARTS = 8
X_CHIPS = 4
BYTES = 576
WIDTH = 128
CHUNKS = ((0, 128), (128, 128), (256, 128), (384, 48))
LOW = -1e30
XBC = INNER + 2 * N
VMEM_LIMIT = 24 * 2**20
eps = 1e-05
F32 = jnp.float32
BF16 = jnp.bfloat16


def dot(a, b, contract=((1,), (0,))):
    return lax.dot_general(a, b, (contract, ((), ())), preferred_element_type=F32)


def halves(a):
    hi = a.astype(BF16)
    return hi, (a - hi.astype(F32)).astype(BF16)


def thirds(a):
    hi = a.astype(BF16)
    rest = a - hi.astype(F32)
    mid = rest.astype(BF16)
    return hi, mid, (rest - mid.astype(F32)).astype(BF16)


def dot3(a, b, contract=((1,), (0,))):
    a_hi, a_lo = halves(a)
    b_hi, b_lo = halves(b)
    return dot(a_hi, b_hi, contract) + dot(a_hi, b_lo, contract) + dot(a_lo, b_hi, contract)


def iota(shape, dim):
    return lax.broadcasted_iota(jnp.int32, shape, dim)


def spread_heads(a):
    owner = (iota((2 * HEADS_HERE, INNER), 1) // P_SIZE) == (
        iota((2 * HEADS_HERE, INNER), 0) % HEADS_HERE
    )
    hi, lo = halves(a)
    return dot(jnp.concatenate([hi, lo], axis=1), owner.astype(BF16))


def line(ref):
    return ref[...].reshape(1, ref.shape[0])


def fetch(given, held, sems, first=0):
    copies = [
        pltpu.make_async_copy(a, b, sems.at[first + i]) for i, (a, b) in enumerate(zip(given, held))
    ]
    for copy in copies:
        copy.start()
    return copies


def arrived(copies):
    for copy in copies:
        copy.wait()


def select_kernel(flags_hbm, enc_hbm, packed_ref, flags_ref, enc_ref, sems):
    copies = fetch((flags_hbm, enc_hbm), (flags_ref, enc_ref), sems)
    arrived(copies)
    flags = line(flags_ref)
    upper = (iota((BYTES, BYTES), 0) <= iota((BYTES, BYTES), 1)).astype(BF16)
    rank = dot(flags.astype(F32).astype(BF16), upper)
    place = jnp.where(flags > 0, rank.astype(jnp.int32) - 1, -1)
    hit = (iota((CAP, BYTES), 0) == place).astype(F32).astype(BF16)
    packed_ref[...] = dot(hit, enc_ref[...]).astype(BF16)


def weights_kernel(flags_ref, prob_ref, packed_ref, w_hi_ref, w_lo_ref, carry_ref, own_ref, decay_ref):
    flags = line(flags_ref).astype(F32)
    prob = prob_ref[...].astype(F32).reshape(1, BYTES)
    logs = jnp.where(flags > 0, jnp.log1p(-prob), 0.0)
    before = iota((BYTES, BYTES), 1) <= iota((BYTES, BYTES), 0)
    after = iota((BYTES, BYTES), 0) <= iota((BYTES, BYTES), 1)
    same = iota((BYTES, BYTES), 1) == iota((BYTES, BYTES), 0)

    def column(mask, row):
        return jnp.sum(jnp.where(mask, row, 0.0), axis=1, keepdims=True)

    def across(mask, col):
        return jnp.sum(jnp.where(mask, col, 0.0), axis=0, keepdims=True)

    rank = column(before, flags)
    kept = column(before, logs)
    flag = column(same, flags)
    chance = column(same, prob)
    place = iota((BYTES, CAP), 1).astype(F32)
    hit = (place == rank - 1.0) & (flag > 0)
    gap = jnp.where(place < rank, kept - across(hit, kept), LOW)
    hi, lo = halves(jnp.exp(gap) * across(hit, chance))
    w_hi_ref[...] = hi
    w_lo_ref[...] = lo
    decay_ref[...] = jnp.exp(kept)
    rank_row = across(after, flag)
    kept_row = across(after, column(same, logs))
    place = iota((CAP, BYTES), 0).astype(F32)
    hit = (place == rank_row - 1.0) & (flags > 0)
    total = jnp.sum(logs, axis=1, keepdims=True)
    count = jnp.sum(flags, axis=1, keepdims=True)
    real = iota((CAP, 1), 0).astype(F32) < count
    weight = jnp.exp(jnp.where(real, total - column(hit, kept_row), LOW)) * column(hit, prob)
    wide = jnp.broadcast_to(weight, (CAP, WIDTH))
    carry_ref[...] = wide
    own_ref[...] = jnp.sum(wide * packed_ref[...].astype(F32), axis=0, keepdims=True)


def log_decays(step, a_log_ref):
    return -jnp.exp(line(a_log_ref)) * step


def sum_thirds(sums, axis):
    h = HEADS_HERE
    if axis == 0:
        return sums[:h] + sums[h : 2 * h] + sums[2 * h :]
    return sums[:, :h] + sums[:, h : 2 * h] + sums[:, 2 * h :]


def project_kernel(
    rows_ref, w_in_ref, *refs,
):
    given, refs = refs[:9], refs[9:]
    (xbc_hbm, normed_hbm, aux_hbm, pieces_ref), refs = refs[:4], refs[4:]
    held, (xbc_ref, normed_ref, aux_ref, w_ref, sems, small_sems, out_sems) = refs[:9], refs[9:]
    flags_ref, prob_ref, pad_ref, gain_ref, w_dt_ref, pad_proj_ref, pad_dt_ref, bias_ref, a_log_ref = held
    small = fetch(given, held, small_sems)
    tiles = range(XBC // 256)
    copies = [
        pltpu.make_async_copy(
            w_in_ref.at[:, INNER + 256 * t : INNER + 256 * (t + 1)], w_ref.at[t], sems.at[t]
        )
        for t in tiles
    ]
    for copy in copies:
        copy.start()
    energy = jnp.zeros((CAP, WIDTH), F32)
    for i in range(HEAD_PARTS):
        wide = rows_ref[:, i * WIDTH : (i + 1) * WIDTH].astype(F32)
        energy = energy + wide * wide
    arrived(small)
    pad = line(pad_ref)
    power = jnp.sum(energy, axis=1, keepdims=True) + jnp.sum(pad * pad)
    inverse = lax.rsqrt(power / E + eps)
    gain = line(gain_ref)
    for i in range(HEAD_PARTS):
        lanes = slice(i * WIDTH, (i + 1) * WIDTH)
        normed_ref[:, lanes] = (rows_ref[:, lanes].astype(F32) * inverse * gain[:, lanes]).astype(BF16)
    kept = [pltpu.make_async_copy(normed_ref, normed_hbm, out_sems.at[0])]
    kept[0].start()
    h = HEADS_HERE
    raw = dot(normed_ref[...], w_dt_ref[...], ((1,), (1,))) + inverse * line(pad_dt_ref) + line(bias_ref)
    soft = jnp.maximum(raw, 0.0) + jnp.log1p(jnp.exp(-jnp.abs(raw)))
    count = jnp.sum(line(flags_ref).astype(F32), axis=1, keepdims=True)
    step = jnp.where(iota((CAP, h), 0).astype(F32) < count, soft, 0.0)
    split = jnp.concatenate(thirds(log_decays(step, a_log_ref)), axis=1)
    lower = (iota((CAP, CAP), 1) <= iota((CAP, CAP), 0)).astype(BF16)
    run = sum_thirds(dot(lower, split), 1)
    fill = jnp.zeros((CAP, WIDTH - 2 * h - 1), F32)
    aux_ref[...] = jnp.concatenate([step, run, inverse, fill], axis=1)
    total = run[CAP - 1 :, :]
    tail = spread_heads(jnp.exp(total - run) * step)
    pad_proj = line(pad_proj_ref)
    for t in tiles:
        copies[t].wait()
        lanes = slice(256 * t, 256 * (t + 1))
        offset = inverse * pad_proj[:, INNER + 256 * t : INNER + 256 * (t + 1)]
        xbc_ref[:, lanes] = dot(normed_ref[...], w_ref[t]) + offset
    kept += fetch((xbc_ref, aux_ref), (xbc_hbm, aux_hbm), out_sems, 1)
    state = dot3(xbc_ref[:, INNER : INNER + N], xbc_ref[:, :INNER] * tail, ((0,), (0,)))
    prob = prob_ref[...].astype(F32).reshape(1, BYTES)
    keeps = jnp.sum(jnp.where(line(flags_ref) > 0, jnp.log1p(-prob), 0.0), axis=1, keepdims=True)
    head_row = jnp.concatenate([total, jnp.zeros((1, WIDTH - h), F32)], axis=1)
    spare = jnp.concatenate(
        [head_row, jnp.broadcast_to(keeps, (1, WIDTH)), jnp.zeros((2, WIDTH), F32)], axis=0
    )
    parts = pieces_ref.shape[0]
    per = N // parts
    for d in range(parts):
        pieces_ref[d, :, :INNER] = state[d * per : (d + 1) * per, :]
        pieces_ref[d, 0:4, INNER:] = spare
        if per > 4:
            pieces_ref[d, 4:, INNER:] = jnp.zeros((per - 4, WIDTH), F32)
    arrived(kept)


def local_kernel(*refs):
    given, w_in_ref, outs_hbm, held = refs[:6], refs[6], refs[7:9], refs[9:15]
    out_ref, silu_ref, w_ref, sems, out_sems = refs[15:]
    xbc_ref, normed_ref, aux_ref, pad_proj_ref, a_log_ref, skip_ref = held
    h = HEADS_HERE
    tiles = range(INNER // 256)
    pieces = [w_in_ref.at[:, 256 * t : 256 * (t + 1)] for t in tiles]
    copies = fetch(given + tuple(pieces), held + tuple(w_ref.at[t] for t in tiles), sems)
    arrived(copies[: len(held)])
    copies = copies[len(held) :]
    split = jnp.concatenate(thirds(log_decays(aux_ref[:, :h], a_log_ref)), axis=1)
    upper = (iota((CAP, CAP), 0) <= iota((CAP, CAP), 1)).astype(BF16)
    run_t = sum_thirds(dot(split, upper, ((0,), (0,))), 0)
    state = jnp.zeros((N, INNER), F32)
    skip = spread_heads(jnp.broadcast_to(line(skip_ref), (8, HEADS_HERE)))[0:1, :]
    start_run = jnp.zeros((1, HEADS_HERE), F32)
    for start, length in CHUNKS:
        rows = slice(start, start + length)
        x = xbc_ref[rows, :INNER]
        b = xbc_ref[rows, INNER : INNER + N]
        c = xbc_ref[rows, INNER + N :]
        step = aux_ref[rows, :h]
        run = aux_ref[rows, h : 2 * h]
        end_run = run[length - 1 :, :]
        scaled = (x * spread_heads(step)).astype(BF16)
        inter = dot3(c, b, ((1,), (1,)))
        lower = iota((length, length), 0) >= iota((length, length), 1)
        outs = []
        for k in range(HEADS_HERE):
            gap = run[:, k : k + 1] - run_t[k : k + 1, rows]
            w = inter * jnp.exp(jnp.where(lower, gap, LOW))
            outs.append(dot(w.astype(BF16), scaled[:, k * P_SIZE : (k + 1) * P_SIZE]))
        y = jnp.concatenate(outs, axis=1) + skip * x
        if start > 0:
            y = y + spread_heads(jnp.exp(run - start_run)) * dot3(c, state)
        out_ref[rows, :] = y.astype(BF16)
        if start + length < CAP:
            weighted = x * spread_heads(step * jnp.exp(end_run - run))
            kept = spread_heads(jnp.broadcast_to(jnp.exp(end_run - start_run), (8, HEADS_HERE)))
            state = state * kept[0:1, :] + dot3(b, weighted, ((0,), (0,)))
        start_run = end_run
    kept = fetch((out_ref,), outs_hbm[:1], out_sems)
    pad_proj = line(pad_proj_ref)
    inverse = aux_ref[:, 2 * h : 2 * h + 1]
    for t in range(INNER // 256):
        copies[t].wait()
        lanes = slice(256 * t, 256 * (t + 1))
        gate = dot(normed_ref[...], w_ref[t]) + inverse * pad_proj[:, lanes]
        silu_ref[:, lanes] = (gate / (1.0 + jnp.exp(-gate))).astype(BF16)
    kept += fetch((silu_ref,), outs_hbm[1:], out_sems, 1)
    arrived(kept)


def scan_kernel(got_ref, before_ref, keeps_ref):
    act, per, _ = got_ref.shape
    logs = jnp.concatenate([got_ref[j, 0:1, INNER:] for j in range(act)], axis=0)
    keeps_ref[...] = jnp.concatenate([got_ref[j, 1:2, INNER:] for j in range(act)], axis=0)
    keep = spread_heads(jnp.exp(logs[:, :HEADS_HERE]))
    state = jnp.zeros((per, INNER), F32)
    for j in range(act):
        before_ref[j] = state
        state = state * keep[j : j + 1, :] + got_ref[j, :, :INNER]


def output_kernel(
    state_ref, c_hbm, aux_hbm, local_hbm, silu_hbm, gain_hbm, w_out_hbm, carry_hbm, own_hbm,
    kept_ref, sent_ref, rows_ref,
    full_ref, c_ref, aux_ref, local_ref, silu_ref, gain_ref, w_ref, carry_ref, own_ref, sems,
):
    core = lax.axis_index("core")
    head = lax.axis_index("x") * 2 + core
    copies = fetch(
        (c_hbm.at[:, INNER + N :], aux_hbm, local_hbm, silu_hbm, gain_hbm, w_out_hbm, carry_hbm, own_hbm),
        (c_ref, aux_ref, local_ref, silu_ref, gain_ref, w_ref, carry_ref, own_ref),
        sems,
    )
    parts, per, _ = state_ref.shape
    for d in range(parts):
        full_ref[d * per : (d + 1) * per, :] = state_ref[d]
    arrived(copies[:2])
    carried = spread_heads(jnp.exp(aux_ref[:, HEADS_HERE : 2 * HEADS_HERE])) * dot3(c_ref[...], full_ref[...])
    arrived(copies[2:5])
    gated = (local_ref[...].astype(F32) + carried) * silu_ref[...].astype(F32)
    power = jnp.mean(gated * gated, axis=1, keepdims=True)
    mixed = (gated * lax.rsqrt(power + eps) * line(gain_ref)).astype(BF16)
    arrived(copies[5:])
    weight = carry_ref[...]
    carries = []
    for i in range(X_CHIPS):
        pair = dot(mixed, w_ref[:, i * 2 * WIDTH : (i + 1) * 2 * WIDTH])
        first, second = pair[:, :WIDTH], pair[:, WIDTH:]
        kept_ref[i] = jnp.where(core == 0, first, second)
        sent_ref[i] = jnp.where(core == 0, second, first).astype(BF16)
        carries += [jnp.sum(weight * part, axis=0, keepdims=True) for part in (first, second)]
    mine = iota((HEAD_PARTS, WIDTH), 0) == head
    rows = jnp.concatenate(carries, axis=0) + jnp.where(mine, own_ref[...], 0.0)
    rows_ref[...] = jnp.broadcast_to(rows[None], rows_ref.shape)


def pair_kernel(packed_ref, own_ref, got_ref, keep_ref, s1, s2, s3):
    x = lax.axis_index("x")
    keep_ref[...] = packed_ref[...].astype(F32) + (own_ref[x] + got_ref[x].astype(F32))
    for s, out_ref in enumerate((s1, s2, s3), start=1):
        chip = lax.rem(x + s, X_CHIPS)
        out_ref[...] = (own_ref[chip] + got_ref[chip].astype(F32)).astype(BF16)


def carry_kernel(got_ref, keeps_ref, sent_ref):
    me = lax.axis_index("act")
    act, parts, _ = got_ref.shape
    keep = jnp.exp(keeps_ref[...])
    carry = jnp.zeros((parts, WIDTH), F32)
    for j in range(act):
        carry = jnp.where(j < me, carry * keep[j : j + 1, :] + got_ref[j], carry)
    for i in range(parts):
        sent_ref[i] = carry[i : i + 1, :]


def decode_kernel(enc_ref, w_hi_ref, w_lo_ref, keep_ref, r1, r2, r3, decay_ref, carries_ref, out_ref):
    added = r1[...].astype(F32) + r2[...].astype(F32) + r3[...].astype(F32)
    main = (keep_ref[...] + added).astype(BF16)
    carry = carries_ref[0]
    for i in range(1, HEAD_PARTS):
        carry = carry + carries_ref[i]
    smoothed = dot(w_hi_ref[...], main) + dot(w_lo_ref[...], main) + decay_ref[...] * carry
    out_ref[...] = (enc_ref[...].astype(F32) + smoothed).astype(BF16)


def shape(dims, dtype=F32):
    return jax.ShapeDtypeStruct(dims, dtype)


def call(kernel, outs, name, specs=None, out_specs=None, scratch=(), flops=0, transcendentals=0, nbytes=0):
    more = {} if specs is None else {"in_specs": specs}
    if out_specs is not None:
        more["out_specs"] = out_specs
    run = pl.pallas_call(
        kernel,
        out_shape=outs,
        name=name,
        scratch_shapes=scratch,
        compiler_params=pltpu.CompilerParams(vmem_limit_bytes=VMEM_LIMIT),
        cost_estimate=pl.CostEstimate(
            flops=flops, transcendentals=transcendentals, bytes_accessed=nbytes
        ),
        **more,
    )
    if specs is None:
        return run
    return lambda *args: run(
        *[
            pltpu.with_memory_space_constraint(a, pltpu.HBM) if spec.memory_space == pltpu.HBM else a
            for a, spec in zip(args, specs)
        ]
    )


def body(
    enc_rows,
    boundary_flags,
    boundary_prob,
    pad_vector,
    norm_gain,
    w_in,
    w_dt,
    pad_proj,
    pad_dt,
    dt_bias,
    a_log,
    d_skip,
    gate_gain,
    w_out,
):
    act = lax.axis_size("act")
    heads = ("x", "core")
    held, apart = pl.BlockSpec(), pl.BlockSpec(memory_space=pltpu.HBM)
    dma = pltpu.SemaphoreType.DMA
    packed = call(
        select_kernel,
        shape((CAP, WIDTH), BF16),
        "select",
        specs=[apart] * 2,
        scratch=[pltpu.VMEM((BYTES,), jnp.int32), pltpu.VMEM((BYTES, WIDTH), BF16), dma((2,))],
        flops=10**8,
    )(boundary_flags, enc_rows)
    rows = lax.all_gather(packed, heads, axis=1, tiled=True)

    w_hi, w_lo, carry_w, own_row, decay = call(
        weights_kernel,
        (
            shape((BYTES, CAP), BF16),
            shape((BYTES, CAP), BF16),
            shape((CAP, WIDTH)),
            shape((1, WIDTH)),
            shape((BYTES, 1)),
        ),
        "weights",
        transcendentals=BYTES * CAP,
        flops=BYTES * CAP * 30,
        nbytes=10**6,
    )(boundary_flags, boundary_prob, packed)

    small = [boundary_flags, boundary_prob, pad_vector, norm_gain, w_dt.T, pad_proj, pad_dt, dt_bias, a_log]
    kept_across = [((CAP, XBC), F32), ((CAP, D), BF16), ((CAP, WIDTH), F32)]
    xbc, normed, aux, pieces = call(
        project_kernel,
        [pltpu.HBM(*a) for a in kept_across] + [shape((act, N // act, INNER + WIDTH))],
        "project",
        out_specs=[apart] * 3 + [held],
        specs=[held] + [apart] * (1 + len(small)),
        scratch=[pltpu.VMEM(a.shape, a.dtype) for a in small]
        + [pltpu.VMEM(*a) for a in kept_across]
        + [pltpu.VMEM((XBC // 256, D, 256), BF16), dma((XBC // 256,)), dma((len(small),)), dma((3,))],
        flops=2 * CAP * D * XBC,
        nbytes=8 * 10**6,
    )(rows, w_in, *small)

    got = lax.all_to_all(pieces, "act", 0, 0)
    needed = [xbc, normed, aux, pad_proj, a_log, d_skip]
    local, silu = call(
        local_kernel,
        [pltpu.HBM((CAP, INNER), BF16)] * 2,
        "local",
        out_specs=[apart] * 2,
        specs=[apart] * (len(needed) + 1),
        scratch=[pltpu.VMEM(a.shape, a.dtype) for a in needed]
        + [pltpu.VMEM((CAP, INNER), BF16)] * 2
        + [pltpu.VMEM((INNER // 256, D, 256), BF16), dma((len(needed) + INNER // 256,)), dma((2,))],
        flops=2 * 10**9,
        transcendentals=CAP * 2048,
        nbytes=6 * 10**6,
    )(*needed, w_in)
    before, keeps = call(
        scan_kernel, (shape((act, N // act, INNER)), shape((act, WIDTH))), "scan", nbytes=6 * 10**5
    )(got)
    state_in = lax.all_to_all(before, "act", 0, 0)

    own, sent, carry_rows = call(
        output_kernel,
        (
            shape((X_CHIPS, CAP, WIDTH)),
            shape((X_CHIPS, CAP, WIDTH), BF16),
            shape((act, HEAD_PARTS, WIDTH)),
        ),
        "output",
        specs=[held] + [apart] * 8,
        scratch=[
            pltpu.VMEM((N, INNER), F32),
            pltpu.VMEM((CAP, N), F32),
            pltpu.VMEM((CAP, WIDTH), F32),
            pltpu.VMEM((CAP, INNER), BF16),
            pltpu.VMEM((CAP, INNER), BF16),
            pltpu.VMEM((INNER,), F32),
            pltpu.VMEM((INNER, D), BF16),
            pltpu.VMEM((CAP, WIDTH), F32),
            pltpu.VMEM((1, WIDTH), F32),
            dma((8,)),
        ],
        flops=2 * CAP * INNER * D,
        nbytes=6 * 10**6,
    )(state_in, xbc, aux, local, silu, gate_gain, w_out, carry_w, own_row)

    all_rows = lax.all_to_all(carry_rows, "act", 0, 0)
    got_sums = lax.ppermute(sent, "core", [(0, 1), (1, 0)])
    block = shape((CAP, WIDTH), BF16)
    keep, *parts = call(
        pair_kernel, (shape((CAP, WIDTH)), block, block, block), "pair", nbytes=2 * 10**6
    )(packed, own, got_sums)
    parts = [over_chips(a, s) for s, a in enumerate(parts, start=1)]
    carry = call(carry_kernel, shape((HEAD_PARTS, 1, WIDTH)), "carry", nbytes=2 * 10**5)(all_rows, keeps)
    carries = lax.all_to_all(carry, heads, 0, 0)
    return call(
        decode_kernel, shape((BYTES, WIDTH), BF16), "decode", flops=2 * 10**8, nbytes=2 * 10**6
    )(enc_rows, w_hi, w_lo, keep, *parts, decay, carries)


def over_chips(a, s):
    return lax.ppermute(a, "x", [(i, (i + s) % X_CHIPS) for i in range(X_CHIPS)])


def solution(mesh):
    seq = mesh.shape["seq"]
    split = Mesh(mesh.devices.reshape(2, seq // 2, X_CHIPS, 2), ("half", "act", "x", "core"))
    by_seq, by_head = ("half", "act"), ("x", "core")
    in_specs = (
        P(by_seq, by_head),
        P(by_seq),
        P(by_seq),
        P(),
        P(),
        P(None, by_head),
        P(None, by_head),
        P(by_head),
        P(by_head),
        P(by_head),
        P(by_head),
        P(by_head),
        P(by_head),
        P(by_head, None),
    )
    return jax.shard_map(
        body, mesh=split, in_specs=in_specs, out_specs=P(by_seq, by_head), check_vma=False
    )
```

```python
import jax
import jax.numpy as jnp
from jax import lax
from jax.experimental import pallas as pl
from jax.experimental.pallas import tpu as pltpu
from jax.sharding import Mesh
from jax.sharding import PartitionSpec as P

D = 1024
E = 2048
N = 128
HEADS_HERE = 8
P_SIZE = 64
INNER = HEADS_HERE * P_SIZE
COLS = 2 * INNER + 2 * N
CAP = 432
HEAD_PARTS = 8
X_CHIPS = 4
BYTES = 576
WIDTH = 128
CHUNKS = ((0, 128), (128, 128), (256, 128), (384, 48))
LOW = -1e30
XBC = INNER + 2 * N
VMEM_LIMIT = 24 * 2**20
eps = 1e-05
F32 = jnp.float32
BF16 = jnp.bfloat16


def dot(a, b, contract=((1,), (0,))):
    return lax.dot_general(a, b, (contract, ((), ())), preferred_element_type=F32)


def halves(a):
    hi = a.astype(BF16)
    return hi, (a - hi.astype(F32)).astype(BF16)


def thirds(a):
    hi = a.astype(BF16)
    rest = a - hi.astype(F32)
    mid = rest.astype(BF16)
    return hi, mid, (rest - mid.astype(F32)).astype(BF16)


def dot3(a, b, contract=((1,), (0,))):
    a_hi, a_lo = halves(a)
    b_hi, b_lo = halves(b)
    return dot(a_hi, b_hi, contract) + dot(a_hi, b_lo, contract) + dot(a_lo, b_hi, contract)


def iota(shape, dim):
    return lax.broadcasted_iota(jnp.int32, shape, dim)


def spread_heads(a):
    owner = (iota((2 * HEADS_HERE, INNER), 1) // P_SIZE) == (
        iota((2 * HEADS_HERE, INNER), 0) % HEADS_HERE
    )
    hi, lo = halves(a)
    return dot(jnp.concatenate([hi, lo], axis=1), owner.astype(BF16))


def line(ref):
    return ref[...].reshape(1, ref.shape[0])


def fetch(given, held, sems, first=0):
    copies = [
        pltpu.make_async_copy(a, b, sems.at[first + i]) for i, (a, b) in enumerate(zip(given, held))
    ]
    for copy in copies:
        copy.start()
    return copies


def arrived(copies):
    for copy in copies:
        copy.wait()


def select_kernel(flags_hbm, enc_hbm, packed_ref, flags_ref, enc_ref, sems):
    copies = fetch((flags_hbm, enc_hbm), (flags_ref, enc_ref), sems)
    arrived(copies)
    flags = line(flags_ref)
    upper = (iota((BYTES, BYTES), 0) <= iota((BYTES, BYTES), 1)).astype(BF16)
    rank = dot(flags.astype(F32).astype(BF16), upper)
    place = jnp.where(flags > 0, rank.astype(jnp.int32) - 1, -1)
    hit = (iota((CAP, BYTES), 0) == place).astype(F32).astype(BF16)
    packed_ref[...] = dot(hit, enc_ref[...]).astype(BF16)


def weights_kernel(flags_ref, prob_ref, packed_ref, w_hi_ref, w_lo_ref, carry_ref, own_ref, decay_ref):
    flags = line(flags_ref).astype(F32)
    prob = prob_ref[...].astype(F32).reshape(1, BYTES)
    logs = jnp.where(flags > 0, jnp.log1p(-prob), 0.0)
    before = iota((BYTES, BYTES), 1) <= iota((BYTES, BYTES), 0)
    after = iota((BYTES, BYTES), 0) <= iota((BYTES, BYTES), 1)
    same = iota((BYTES, BYTES), 1) == iota((BYTES, BYTES), 0)

    def column(mask, row):
        return jnp.sum(jnp.where(mask, row, 0.0), axis=1, keepdims=True)

    def across(mask, col):
        return jnp.sum(jnp.where(mask, col, 0.0), axis=0, keepdims=True)

    rank = column(before, flags)
    kept = column(before, logs)
    flag = column(same, flags)
    chance = column(same, prob)
    place = iota((BYTES, CAP), 1).astype(F32)
    hit = (place == rank - 1.0) & (flag > 0)
    gap = jnp.where(place < rank, kept - across(hit, kept), LOW)
    hi, lo = halves(jnp.exp(gap) * across(hit, chance))
    w_hi_ref[...] = hi
    w_lo_ref[...] = lo
    decay_ref[...] = jnp.exp(kept)
    rank_row = across(after, flag)
    kept_row = across(after, column(same, logs))
    place = iota((CAP, BYTES), 0).astype(F32)
    hit = (place == rank_row - 1.0) & (flags > 0)
    total = jnp.sum(logs, axis=1, keepdims=True)
    count = jnp.sum(flags, axis=1, keepdims=True)
    real = iota((CAP, 1), 0).astype(F32) < count
    weight = jnp.exp(jnp.where(real, total - column(hit, kept_row), LOW)) * column(hit, prob)
    wide = jnp.broadcast_to(weight, (CAP, WIDTH))
    carry_ref[...] = wide
    own_ref[...] = jnp.sum(wide * packed_ref[...].astype(F32), axis=0, keepdims=True)


def log_decays(step, a_log_ref):
    return -jnp.exp(line(a_log_ref)) * step


def sum_thirds(sums, axis):
    h = HEADS_HERE
    if axis == 0:
        return sums[:h] + sums[h : 2 * h] + sums[2 * h :]
    return sums[:, :h] + sums[:, h : 2 * h] + sums[:, 2 * h :]


def project_kernel(
    rows_ref, w_in_ref, *refs,
):
    given, refs = refs[:9], refs[9:]
    (xbc_hbm, normed_hbm, aux_hbm, pieces_ref), refs = refs[:4], refs[4:]
    held, (xbc_ref, normed_ref, aux_ref, w_ref, sems, small_sems, out_sems) = refs[:9], refs[9:]
    flags_ref, prob_ref, pad_ref, gain_ref, w_dt_ref, pad_proj_ref, pad_dt_ref, bias_ref, a_log_ref = held
    small = fetch(given, held, small_sems)
    tiles = range(XBC // 256)
    copies = [
        pltpu.make_async_copy(
            w_in_ref.at[:, INNER + 256 * t : INNER + 256 * (t + 1)], w_ref.at[t], sems.at[t]
        )
        for t in tiles
    ]
    for copy in copies:
        copy.start()
    energy = jnp.zeros((CAP, WIDTH), F32)
    for i in range(HEAD_PARTS):
        wide = rows_ref[:, i * WIDTH : (i + 1) * WIDTH].astype(F32)
        energy = energy + wide * wide
    arrived(small)
    pad = line(pad_ref)
    power = jnp.sum(energy, axis=1, keepdims=True) + jnp.sum(pad * pad)
    inverse = lax.rsqrt(power / E + eps)
    gain = line(gain_ref)
    for i in range(HEAD_PARTS):
        lanes = slice(i * WIDTH, (i + 1) * WIDTH)
        normed_ref[:, lanes] = (rows_ref[:, lanes].astype(F32) * inverse * gain[:, lanes]).astype(BF16)
    kept = [pltpu.make_async_copy(normed_ref, normed_hbm, out_sems.at[0])]
    kept[0].start()
    h = HEADS_HERE
    raw = dot(normed_ref[...], w_dt_ref[...], ((1,), (1,))) + inverse * line(pad_dt_ref) + line(bias_ref)
    soft = jnp.maximum(raw, 0.0) + jnp.log1p(jnp.exp(-jnp.abs(raw)))
    count = jnp.sum(line(flags_ref).astype(F32), axis=1, keepdims=True)
    step = jnp.where(iota((CAP, h), 0).astype(F32) < count, soft, 0.0)
    split = jnp.concatenate(thirds(log_decays(step, a_log_ref)), axis=1)
    lower = (iota((CAP, CAP), 1) <= iota((CAP, CAP), 0)).astype(BF16)
    run = sum_thirds(dot(lower, split), 1)
    fill = jnp.zeros((CAP, WIDTH - 2 * h - 1), F32)
    aux_ref[...] = jnp.concatenate([step, run, inverse, fill], axis=1)
    total = run[CAP - 1 :, :]
    tail = spread_heads(jnp.exp(total - run) * step)
    pad_proj = line(pad_proj_ref)
    for t in tiles:
        copies[t].wait()
        lanes = slice(256 * t, 256 * (t + 1))
        offset = inverse * pad_proj[:, INNER + 256 * t : INNER + 256 * (t + 1)]
        xbc_ref[:, lanes] = dot(normed_ref[...], w_ref[t]) + offset
    kept += fetch((xbc_ref, aux_ref), (xbc_hbm, aux_hbm), out_sems, 1)
    state = dot3(xbc_ref[:, INNER : INNER + N], xbc_ref[:, :INNER] * tail, ((0,), (0,)))
    prob = prob_ref[...].astype(F32).reshape(1, BYTES)
    keeps = jnp.sum(jnp.where(line(flags_ref) > 0, jnp.log1p(-prob), 0.0), axis=1, keepdims=True)
    head_row = jnp.concatenate([total, jnp.zeros((1, WIDTH - h), F32)], axis=1)
    spare = jnp.concatenate(
        [head_row, jnp.broadcast_to(keeps, (1, WIDTH)), jnp.zeros((2, WIDTH), F32)], axis=0
    )
    parts = pieces_ref.shape[0]
    per = N // parts
    for d in range(parts):
        pieces_ref[d, :, :INNER] = state[d * per : (d + 1) * per, :]
        pieces_ref[d, 0:4, INNER:] = spare
        if per > 4:
            pieces_ref[d, 4:, INNER:] = jnp.zeros((per - 4, WIDTH), F32)
    arrived(kept)


def local_kernel(*refs):
    given, w_in_ref, outs_hbm, held = refs[:6], refs[6], refs[7:9], refs[9:15]
    out_ref, silu_ref, w_ref, sems, out_sems = refs[15:]
    xbc_ref, normed_ref, aux_ref, pad_proj_ref, a_log_ref, skip_ref = held
    h = HEADS_HERE
    tiles = range(INNER // 256)
    pieces = [w_in_ref.at[:, 256 * t : 256 * (t + 1)] for t in tiles]
    copies = fetch(given + tuple(pieces), held + tuple(w_ref.at[t] for t in tiles), sems)
    arrived(copies[: len(held)])
    copies = copies[len(held) :]
    split = jnp.concatenate(thirds(log_decays(aux_ref[:, :h], a_log_ref)), axis=1)
    upper = (iota((CAP, CAP), 0) <= iota((CAP, CAP), 1)).astype(BF16)
    run_t = sum_thirds(dot(split, upper, ((0,), (0,))), 0)
    state = jnp.zeros((N, INNER), F32)
    skip = spread_heads(jnp.broadcast_to(line(skip_ref), (8, HEADS_HERE)))[0:1, :]
    start_run = jnp.zeros((1, HEADS_HERE), F32)
    for start, length in CHUNKS:
        rows = slice(start, start + length)
        x = xbc_ref[rows, :INNER]
        b = xbc_ref[rows, INNER : INNER + N]
        c = xbc_ref[rows, INNER + N :]
        step = aux_ref[rows, :h]
        run = aux_ref[rows, h : 2 * h]
        end_run = run[length - 1 :, :]
        scaled = (x * spread_heads(step)).astype(BF16)
        inter = dot3(c, b, ((1,), (1,)))
        lower = iota((length, length), 0) >= iota((length, length), 1)
        outs = []
        for k in range(HEADS_HERE):
            gap = run[:, k : k + 1] - run_t[k : k + 1, rows]
            w = inter * jnp.exp(jnp.where(lower, gap, LOW))
            outs.append(dot(w.astype(BF16), scaled[:, k * P_SIZE : (k + 1) * P_SIZE]))
        y = jnp.concatenate(outs, axis=1) + skip * x
        if start > 0:
            y = y + spread_heads(jnp.exp(run - start_run)) * dot3(c, state)
        out_ref[rows, :] = y.astype(BF16)
        if start + length < CAP:
            weighted = x * spread_heads(step * jnp.exp(end_run - run))
            kept = spread_heads(jnp.broadcast_to(jnp.exp(end_run - start_run), (8, HEADS_HERE)))
            state = state * kept[0:1, :] + dot3(b, weighted, ((0,), (0,)))
        start_run = end_run
    kept = fetch((out_ref,), outs_hbm[:1], out_sems)
    pad_proj = line(pad_proj_ref)
    inverse = aux_ref[:, 2 * h : 2 * h + 1]
    for t in range(INNER // 256):
        copies[t].wait()
        lanes = slice(256 * t, 256 * (t + 1))
        gate = dot(normed_ref[...], w_ref[t]) + inverse * pad_proj[:, lanes]
        silu_ref[:, lanes] = (gate / (1.0 + jnp.exp(-gate))).astype(BF16)
    kept += fetch((silu_ref,), outs_hbm[1:], out_sems, 1)
    arrived(kept)


def scan_kernel(got_ref, before_ref, keeps_hbm, keeps_ref, sems):
    act, per, _ = got_ref.shape
    logs = jnp.concatenate([got_ref[j, 0:1, INNER:] for j in range(act)], axis=0)
    keeps_ref[...] = jnp.concatenate([got_ref[j, 1:2, INNER:] for j in range(act)], axis=0)
    copies = fetch((keeps_ref,), (keeps_hbm,), sems)
    keep = spread_heads(jnp.exp(logs[:, :HEADS_HERE]))
    state = jnp.zeros((per, INNER), F32)
    for j in range(act):
        before_ref[j] = state
        state = state * keep[j : j + 1, :] + got_ref[j, :, :INNER]
    arrived(copies)


def output_kernel(
    state_ref, c_hbm, aux_hbm, local_hbm, silu_hbm, gain_hbm, w_out_hbm, carry_hbm, own_hbm,
    kept_ref, sent_ref, rows_ref,
    full_ref, c_ref, aux_ref, local_ref, silu_ref, gain_ref, w_ref, carry_ref, own_ref, sems,
):
    core = lax.axis_index("core")
    head = lax.axis_index("x") * 2 + core
    copies = fetch(
        (c_hbm.at[:, INNER + N :], aux_hbm, local_hbm, silu_hbm, gain_hbm, w_out_hbm, carry_hbm, own_hbm),
        (c_ref, aux_ref, local_ref, silu_ref, gain_ref, w_ref, carry_ref, own_ref),
        sems,
    )
    parts, per, _ = state_ref.shape
    for d in range(parts):
        full_ref[d * per : (d + 1) * per, :] = state_ref[d]
    arrived(copies[:2])
    carried = spread_heads(jnp.exp(aux_ref[:, HEADS_HERE : 2 * HEADS_HERE])) * dot3(c_ref[...], full_ref[...])
    arrived(copies[2:5])
    gated = (local_ref[...].astype(F32) + carried) * silu_ref[...].astype(F32)
    power = jnp.mean(gated * gated, axis=1, keepdims=True)
    mixed = (gated * lax.rsqrt(power + eps) * line(gain_ref)).astype(BF16)
    arrived(copies[5:])
    weight = carry_ref[...]
    carries = []
    for i in range(X_CHIPS):
        pair = dot(mixed, w_ref[:, i * 2 * WIDTH : (i + 1) * 2 * WIDTH])
        first, second = pair[:, :WIDTH], pair[:, WIDTH:]
        kept_ref[i] = jnp.where(core == 0, first, second)
        sent_ref[i] = jnp.where(core == 0, second, first).astype(BF16)
        carries += [jnp.sum(weight * part, axis=0, keepdims=True) for part in (first, second)]
    mine = iota((HEAD_PARTS, WIDTH), 0) == head
    rows = jnp.concatenate(carries, axis=0) + jnp.where(mine, own_ref[...], 0.0)
    rows_ref[...] = jnp.broadcast_to(rows[None], rows_ref.shape)


def pair_kernel(packed_ref, own_ref, got_ref, keep_ref, s1, s2, s3):
    x = lax.axis_index("x")
    keep_ref[...] = packed_ref[...].astype(F32) + (own_ref[x] + got_ref[x].astype(F32))
    for s, out_ref in enumerate((s1, s2, s3), start=1):
        chip = lax.rem(x + s, X_CHIPS)
        out_ref[...] = (own_ref[chip] + got_ref[chip].astype(F32)).astype(BF16)


def carry_kernel(got_ref, keeps_hbm, sent_ref, keeps_ref, sems):
    me = lax.axis_index("act")
    arrived(fetch((keeps_hbm,), (keeps_ref,), sems))
    act, parts, _ = got_ref.shape
    keep = jnp.exp(keeps_ref[...])
    carry = jnp.zeros((parts, WIDTH), F32)
    for j in range(act):
        carry = jnp.where(j < me, carry * keep[j : j + 1, :] + got_ref[j], carry)
    for i in range(parts):
        sent_ref[i] = carry[i : i + 1, :]


def decode_kernel(enc_ref, w_hi_ref, w_lo_ref, keep_ref, r1, r2, r3, decay_ref, carries_ref, out_ref):
    added = r1[...].astype(F32) + r2[...].astype(F32) + r3[...].astype(F32)
    main = (keep_ref[...] + added).astype(BF16)
    carry = carries_ref[0]
    for i in range(1, HEAD_PARTS):
        carry = carry + carries_ref[i]
    smoothed = dot(w_hi_ref[...], main) + dot(w_lo_ref[...], main) + decay_ref[...] * carry
    out_ref[...] = (enc_ref[...].astype(F32) + smoothed).astype(BF16)


def shape(dims, dtype=F32):
    return jax.ShapeDtypeStruct(dims, dtype)


def call(kernel, outs, name, specs=None, out_specs=None, scratch=(), flops=0, transcendentals=0, nbytes=0):
    more = {} if specs is None else {"in_specs": specs}
    if out_specs is not None:
        more["out_specs"] = out_specs
    run = pl.pallas_call(
        kernel,
        out_shape=outs,
        name=name,
        scratch_shapes=scratch,
        compiler_params=pltpu.CompilerParams(vmem_limit_bytes=VMEM_LIMIT),
        cost_estimate=pl.CostEstimate(
            flops=flops, transcendentals=transcendentals, bytes_accessed=nbytes
        ),
        **more,
    )
    if specs is None:
        return run
    return lambda *args: run(
        *[
            pltpu.with_memory_space_constraint(a, pltpu.HBM) if spec.memory_space == pltpu.HBM else a
            for a, spec in zip(args, specs)
        ]
    )


def body(
    enc_rows,
    boundary_flags,
    boundary_prob,
    pad_vector,
    norm_gain,
    w_in,
    w_dt,
    pad_proj,
    pad_dt,
    dt_bias,
    a_log,
    d_skip,
    gate_gain,
    w_out,
):
    act = lax.axis_size("act")
    heads = ("x", "core")
    held, apart = pl.BlockSpec(), pl.BlockSpec(memory_space=pltpu.HBM)
    dma = pltpu.SemaphoreType.DMA
    packed = call(
        select_kernel,
        shape((CAP, WIDTH), BF16),
        "select",
        specs=[apart] * 2,
        scratch=[pltpu.VMEM((BYTES,), jnp.int32), pltpu.VMEM((BYTES, WIDTH), BF16), dma((2,))],
        flops=10**8,
    )(boundary_flags, enc_rows)
    rows = lax.all_gather(packed, heads, axis=1, tiled=True)

    w_hi, w_lo, carry_w, own_row, decay = call(
        weights_kernel,
        (
            shape((BYTES, CAP), BF16),
            shape((BYTES, CAP), BF16),
            shape((CAP, WIDTH)),
            shape((1, WIDTH)),
            shape((BYTES, 1)),
        ),
        "weights",
        transcendentals=BYTES * CAP,
        flops=BYTES * CAP * 30,
        nbytes=10**6,
    )(boundary_flags, boundary_prob, packed)

    small = [boundary_flags, boundary_prob, pad_vector, norm_gain, w_dt.T, pad_proj, pad_dt, dt_bias, a_log]
    kept_across = [((CAP, XBC), F32), ((CAP, D), BF16), ((CAP, WIDTH), F32)]
    xbc, normed, aux, pieces = call(
        project_kernel,
        [pltpu.HBM(*a) for a in kept_across] + [shape((act, N // act, INNER + WIDTH))],
        "project",
        out_specs=[apart] * 3 + [held],
        specs=[held] + [apart] * (1 + len(small)),
        scratch=[pltpu.VMEM(a.shape, a.dtype) for a in small]
        + [pltpu.VMEM(*a) for a in kept_across]
        + [pltpu.VMEM((XBC // 256, D, 256), BF16), dma((XBC // 256,)), dma((len(small),)), dma((3,))],
        flops=2 * CAP * D * XBC,
        nbytes=8 * 10**6,
    )(rows, w_in, *small)

    got = lax.all_to_all(pieces, "act", 0, 0)
    needed = [xbc, normed, aux, pad_proj, a_log, d_skip]
    local, silu = call(
        local_kernel,
        [pltpu.HBM((CAP, INNER), BF16)] * 2,
        "local",
        out_specs=[apart] * 2,
        specs=[apart] * (len(needed) + 1),
        scratch=[pltpu.VMEM(a.shape, a.dtype) for a in needed]
        + [pltpu.VMEM((CAP, INNER), BF16)] * 2
        + [pltpu.VMEM((INNER // 256, D, 256), BF16), dma((len(needed) + INNER // 256,)), dma((2,))],
        flops=2 * 10**9,
        transcendentals=CAP * 2048,
        nbytes=6 * 10**6,
    )(*needed, w_in)
    before, keeps = call(
        scan_kernel,
        [shape((act, N // act, INNER)), pltpu.HBM((act, WIDTH), F32)],
        "scan",
        specs=[held],
        out_specs=[held, apart],
        scratch=[pltpu.VMEM((act, WIDTH), F32), dma((1,))],
        nbytes=6 * 10**5,
    )(got)
    state_in = lax.all_to_all(before, "act", 0, 0)

    own, sent, carry_rows = call(
        output_kernel,
        (
            shape((X_CHIPS, CAP, WIDTH)),
            shape((X_CHIPS, CAP, WIDTH), BF16),
            shape((act, HEAD_PARTS, WIDTH)),
        ),
        "output",
        specs=[held] + [apart] * 8,
        scratch=[
            pltpu.VMEM((N, INNER), F32),
            pltpu.VMEM((CAP, N), F32),
            pltpu.VMEM((CAP, WIDTH), F32),
            pltpu.VMEM((CAP, INNER), BF16),
            pltpu.VMEM((CAP, INNER), BF16),
            pltpu.VMEM((INNER,), F32),
            pltpu.VMEM((INNER, D), BF16),
            pltpu.VMEM((CAP, WIDTH), F32),
            pltpu.VMEM((1, WIDTH), F32),
            dma((8,)),
        ],
        flops=2 * CAP * INNER * D,
        nbytes=6 * 10**6,
    )(state_in, xbc, aux, local, silu, gate_gain, w_out, carry_w, own_row)

    all_rows = lax.all_to_all(carry_rows, "act", 0, 0)
    got_sums = lax.ppermute(sent, "core", [(0, 1), (1, 0)])
    block = shape((CAP, WIDTH), BF16)
    keep, *parts = call(
        pair_kernel, (shape((CAP, WIDTH)), block, block, block), "pair", nbytes=2 * 10**6
    )(packed, own, got_sums)
    parts = [over_chips(a, s) for s, a in enumerate(parts, start=1)]
    carry = call(
        carry_kernel,
        shape((HEAD_PARTS, 1, WIDTH)),
        "carry",
        specs=[held, apart],
        scratch=[pltpu.VMEM((act, WIDTH), F32), dma((1,))],
        nbytes=2 * 10**5,
    )(all_rows, keeps)
    carries = lax.all_to_all(carry, heads, 0, 0)
    return call(
        decode_kernel, shape((BYTES, WIDTH), BF16), "decode", flops=2 * 10**8, nbytes=2 * 10**6
    )(enc_rows, w_hi, w_lo, keep, *parts, decay, carries)


def over_chips(a, s):
    return lax.ppermute(a, "x", [(i, (i + s) % X_CHIPS) for i in range(X_CHIPS)])


def solution(mesh):
    seq = mesh.shape["seq"]
    split = Mesh(mesh.devices.reshape(2, seq // 2, X_CHIPS, 2), ("half", "act", "x", "core"))
    by_seq, by_head = ("half", "act"), ("x", "core")
    in_specs = (
        P(by_seq, by_head),
        P(by_seq),
        P(by_seq),
        P(),
        P(),
        P(None, by_head),
        P(None, by_head),
        P(by_head),
        P(by_head),
        P(by_head),
        P(by_head),
        P(by_head),
        P(by_head),
        P(by_head, None),
    )
    return jax.shard_map(
        body, mesh=split, in_specs=in_specs, out_specs=P(by_seq, by_head), check_vma=False
    )
```
